32 devices in a mesh: grp: 16 (over z, y, x), tp: 2 (over core).
Axes of the slice: x: 2, y: 2, z: 4, core: 2. Of those that a mesh axis runs over, the one named last changes fastest.
Arguments:
- queries: bfloat16 [128, 2048], P('grp', 'tp'), may hold values from -8 to 8
- new_kv: bfloat16 [128, 2, 512], P('grp', None, 'tp'), may hold values from -6 to 6
- home_cache: bfloat16 [128, 2, 8, 512, 128], P('grp', None, 'tp'), may hold values from -28 to 28
- help_cache: bfloat16 [64, 2, 8, 512, 128], P('grp', None, 'tp'), may hold values from -6 to 6
- lengths: int32 [128], P('grp'), may hold values from 2 to 2048, as said below
- split_at: int32 [128], P('grp'), may hold values from 1 to 1024, as said below
- helper_req: int32 [64], P('grp'), may hold values from 0 to 127, as said below
- out_weight: bfloat16 [2048, 2048], P('tp'), may hold values from -0.125 to 0.125
Outputs:
- attn_out: bfloat16 [128, 2048], P('grp', 'tp')
The draws below stay inside these ranges and needn't reach their ends.
Inputs may be any that keep to these rules, and one draw needn't show every extreme that they name: `lengths`: in each aligned block of 8 requests exactly 4 have more than 1024 cached positions. `split_at`: equal to the length for requests of 1024 positions or fewer; otherwise between length - 1024 and min(1024, length - 1). `helper_req`: groups come in pairs; the 4 helper slots of a group serve, in increasing order, the requests of its partner group that have more than 1024 positions, so each such request has exactly one helper slot and all values are distinct.
All inputs are finite; a program needn't handle non-finite values.
Results may differ from the reference program's by a relative error of at most 0.007.
Values may be sent and summed in bfloat16 or wider, within the bound.
No kernel may reach another device: no remote copies, remote signals or barrier semaphores. Data moves between devices by JAX's collectives and lax.ppermute only.
A program may use at most 192 MiB of HBM per device.

```python
import jax
import jax.numpy as jnp
from jax import lax

D = 2048
H = 32
KVH = 8
HD = 64
CTX = 1024
REQ_G = 8
HELP_G = 4
REQUESTS = 128
HELP = 64


def query_values(key):
    source = jax.random.fold_in(key, 101)
    drawn = jnp.clip(2.0 * jax.random.normal(source, (REQUESTS, H * HD), jnp.float32), -8.0, 8.0)
    return drawn.astype(jnp.bfloat16).astype(jnp.float32)


def draw_queries(key, part):
    return query_values(key).astype(jnp.bfloat16)


def draw_home_cache(key, part):
    shape = (REQUESTS, 2, KVH, CTX // 2, 2 * HD)
    base = jnp.clip(jax.random.normal(jax.random.fold_in(key, 102), shape, jnp.float32), -6.0, 6.0)
    return base.astype(jnp.bfloat16)


def request_plan(key):
    groups = REQUESTS // REQ_G
    group_keys = jax.random.split(jax.random.fold_in(key, 201), groups)
    ranks = jax.vmap(lambda item: jax.random.permutation(item, REQ_G))(group_keys)
    spanning = ranks < HELP_G
    short_len = jax.random.randint(jax.random.fold_in(key, 202), (groups, REQ_G), 2, CTX + 1)
    long_len = jax.random.randint(jax.random.fold_in(key, 203), (groups, REQ_G), CTX + 1, 2 * CTX + 1)
    all_len = jnp.where(spanning, long_len, short_len).reshape(-1)
    span_flat = spanning.reshape(-1)
    forced_group = jax.random.randint(jax.random.fold_in(key, 204), (), 0, groups)
    forced = forced_group * REQ_G + jnp.argmax(ranks[forced_group] == 0).astype(jnp.int32)
    ident = jnp.arange(REQUESTS, dtype=jnp.int32)
    all_len = jnp.where(ident == forced, 2 * CTX, all_len)
    lower = jnp.maximum(all_len - CTX, 1)
    upper = jnp.minimum(CTX, all_len - 1)
    cut_at = jax.random.randint(jax.random.fold_in(key, 205), (REQUESTS,), lower, upper + 1)
    splits = jnp.where(span_flat, cut_at, all_len)
    splits = jnp.where(ident == forced, CTX, splits)
    order = jax.random.permutation(jax.random.fold_in(key, 206), groups)
    places = jnp.argsort(order, stable=True)
    partner = order[jnp.bitwise_xor(places, 1)]
    score_keys = jnp.where(spanning, 0, 1) * REQ_G + jnp.arange(REQ_G, dtype=jnp.int32)[None, :]
    slot_order = jnp.argsort(score_keys, axis=1, stable=True)[:, :HELP_G]
    helpers = (partner[:, None] * REQ_G + slot_order[partner]).reshape(-1)
    return (all_len.astype(jnp.int32), splits.astype(jnp.int32), helpers.astype(jnp.int32))


def draw_lengths(key, part):
    return request_plan(key)[0]


def draw_split_at(key, part):
    return request_plan(key)[1]


def draw_helper_req(key, part):
    return request_plan(key)[2]


def block_levels(key, dims, shards, least, largest):
    def one(position, blocks):
        steps = jax.random.uniform(jax.random.fold_in(jax.random.fold_in(key, 6), position), (blocks,), jnp.float32, least / len(shards), largest / len(shards))
        return jnp.repeat(jnp.exp(steps), dims[position] // blocks).reshape((-1,) + (1,) * (len(dims) - position - 1))

    loudness = one(*shards[0])
    for cut in shards[1:]:
        loudness = loudness * one(*cut)
    return loudness


def bell_draw(rng, dims, deviation, most, pieces=(), held_as=jnp.bfloat16):
    values = deviation * jax.random.normal(rng, dims, jnp.float32)
    if pieces:
        values = values * block_levels(rng, dims, pieces, -0.22, 0.18)
    return jnp.clip(values, -most, most).astype(held_as)


def setup_inputs(seed: int = 0) -> dict:
    streams_of = jax.random.split(jax.random.key(seed), 9)
    queries = draw_queries(jax.random.fold_in(streams_of[8], 71), 0)
    new_kv = bell_draw(streams_of[1], (REQUESTS, 2, KVH * HD), 1.0, 6.0, ((0, 16), (2, 2)))
    home_cache = draw_home_cache(jax.random.fold_in(streams_of[8], 71), 0)
    help_cache = bell_draw(streams_of[3], (HELP, 2, KVH, CTX // 2, 2 * HD), 1.0, 6.0, ((0, 16), (2, 2)))
    lengths = draw_lengths(jax.random.fold_in(streams_of[8], 71), 0)
    split_at = draw_split_at(jax.random.fold_in(streams_of[8], 71), 0)
    helper_req = draw_helper_req(jax.random.fold_in(streams_of[8], 71), 0)
    out_weight = bell_draw(streams_of[7], (H * HD, D), (H * HD) ** -0.5, 0.125, ((0, 2),))
    return {"queries": queries, "new_kv": new_kv, "home_cache": home_cache, "help_cache": help_cache, "lengths": lengths, "split_at": split_at, "helper_req": helper_req, "out_weight": out_weight}


def attend(queries, cache, count, fresh):
    row_count = queries.shape[0]
    kv_heads = cache.shape[2]
    head_width = cache.shape[4] // 2
    context = cache.shape[3] * 2
    group_size = queries.shape[1] // (kv_heads * head_width)
    score_scale = head_width ** -0.5
    head_rows = queries.astype(jnp.float32).reshape(row_count, kv_heads, group_size, head_width)
    key_rows = cache[:, 0].astype(jnp.float32).reshape(row_count, kv_heads, context, head_width)
    value_rows = cache[:, 1].astype(jnp.float32).reshape(row_count, kv_heads, context, head_width)
    scores = jnp.einsum("nkgd,nkpd->nkgp", head_rows, key_rows) * score_scale
    inside = (jnp.arange(context)[None, :] < count[:, None])[:, None, None, :]
    top_score = jnp.max(jnp.where(inside, scores, -1e30), axis=-1)
    if fresh is not None:
        fresh_key = fresh[:, 0].astype(jnp.float32).reshape(row_count, kv_heads, head_width)
        fresh_score = jnp.einsum("nkgd,nkd->nkg", head_rows, fresh_key) * score_scale
        top_score = jnp.maximum(top_score, fresh_score)
    weights = jnp.where(inside, jnp.exp(scores - top_score[..., None]), 0.0).astype(jnp.bfloat16)
    weight_sum = jnp.sum(weights.astype(jnp.float32), axis=-1)
    mixed_sum = jnp.einsum("nkgp,nkpd->nkgd", weights.astype(jnp.float32), value_rows)
    if fresh is not None:
        fresh_weight = lax.optimization_barrier(jnp.exp(fresh_score - top_score).astype(jnp.bfloat16)).astype(jnp.float32)
        weight_sum = weight_sum + fresh_weight
        fresh_value = fresh[:, 1].astype(jnp.float32).reshape(row_count, kv_heads, 1, head_width)
        mixed_sum = mixed_sum + fresh_weight[..., None] * fresh_value
    return (top_score.reshape(row_count, -1), weight_sum.reshape(row_count, -1),
            mixed_sum.reshape(row_count, -1, head_width))


def blocked(queries, cache, count, fresh, blocks):
    def shape_in(array):
        return array.reshape((blocks, array.shape[0] // blocks) + array.shape[1:])

    def flat_out(array):
        return array.reshape((array.shape[0] * array.shape[1],) + array.shape[2:])

    if fresh is None:
        parts = lax.map(lambda items: attend(items[0], items[1], items[2], None),
                        (shape_in(queries), shape_in(cache), shape_in(count)))
    else:
        parts = lax.map(lambda items: attend(items[0], items[1], items[2], items[3]),
                        (shape_in(queries), shape_in(cache), shape_in(count), shape_in(fresh)))
    return flat_out(parts[0]), flat_out(parts[1]), flat_out(parts[2])


def reference(queries, new_kv, home_cache, help_cache, lengths, split_at, helper_req, out_weight):
    blocks = REQUESTS // REQ_G
    home_m, home_l, home_u = blocked(queries, home_cache, split_at, new_kv, blocks)
    help_count = (lengths[helper_req] - split_at[helper_req]).astype(jnp.int32)
    help_m, help_l, help_u = blocked(queries[helper_req], help_cache, help_count, None, blocks)
    far_m = jnp.full(home_m.shape, -1e30, jnp.float32).astype(home_m.dtype).at[helper_req].set(help_m)
    far_l = jnp.zeros_like(home_l).at[helper_req].set(help_l)
    far_u = jnp.zeros_like(home_u).at[helper_req].set(help_u)
    top_score = jnp.maximum(home_m, far_m)
    home_e = jnp.exp(home_m - top_score)
    far_e = jnp.exp(far_m - top_score)
    numerator = home_u * home_e[..., None] + far_u * far_e[..., None]
    denominator = home_l * home_e + far_l * far_e
    mix = (numerator / denominator[..., None]).reshape(REQUESTS, H * HD).astype(jnp.bfloat16)
    return jnp.dot(mix, out_weight, preferred_element_type=jnp.float32).astype(jnp.bfloat16)
```

```python
import jax
import jax.numpy as jnp
from jax import lax
from jax.experimental import pallas as pl
from jax.experimental.pallas import tpu as pltpu
from jax.sharding import PartitionSpec as P

GROUP = 4
HD = 64
LANES = 2 * HD
CTX = 1024
LOW = -1e30
MIB = 1 << 20
MAX_BRANCHES = 32

VMEM = pl.BlockSpec(memory_space=pltpu.VMEM)
SMEM = pl.BlockSpec(memory_space=pltpu.SMEM)
ANY = pl.BlockSpec(memory_space=pl.ANY)


def long_rows(lengths, rows, slots):
    found = jnp.int32(0)
    picks = [jnp.int32(0)] * slots
    for r in range(rows):
        is_long = lengths[r] > CTX
        for k in range(slots):
            picks[k] = jnp.where(jnp.logical_and(is_long, found == k), jnp.int32(r), picks[k])
        found = found + is_long.astype(jnp.int32)
    return picks


def halves(x):
    low = lax.broadcasted_iota(jnp.int32, x.shape, x.ndim - 1) < HD
    swapped = pltpu.roll(x, HD, x.ndim - 1)
    return (
        (jnp.where(low, x, 0.0), jnp.where(low, 0.0, swapped)),
        (jnp.where(low, swapped, 0.0), jnp.where(low, 0.0, x)),
    )


def place_queries(x, q_scr, kv_heads):
    for j in range(kv_heads * GROUP // 2):
        block = halves(x[:, j * LANES : (j + 1) * LANES] * (HD**-0.5))
        for b in range(2):
            kv, i = divmod(2 * j + b, GROUP)
            for parity in range(2):
                q_scr[pl.ds((kv * 8 + parity * 4 + i) * 8, 8), :] = block[b][parity]


def one_slot(q_scr, k_buf, v_buf, e_scr, m_scr, l_scr, slot, count, kv_heads):
    pack = 2 if kv_heads % 2 == 0 else 1
    context = k_buf.shape[1]
    rows = 8 * pack
    shape = (rows, context)
    parity = (lax.broadcasted_iota(jnp.int32, shape, 0) // 4) % 2
    inside = 2 * lax.broadcasted_iota(jnp.int32, shape, 1) + parity < count
    for first in range(0, kv_heads, pack):
        heads = range(first, first + pack)
        blocks = []
        for h in heads:
            part = q_scr[pl.ds(h * 64 + slot, 8, stride=8), :]
            zero = jnp.zeros_like(part)
            blocks.append(jnp.concatenate([part if o == h else zero for o in heads], axis=1))
        q = jnp.concatenate(blocks, axis=0).astype(jnp.bfloat16)
        keys = jnp.concatenate([k_buf[h] for h in heads], axis=1)
        values = jnp.concatenate([v_buf[h] for h in heads], axis=1)
        s = lax.dot_general(q, keys, (((1,), (1,)), ((), ())), preferred_element_type=jnp.float32)
        s = jnp.where(inside, s, LOW)
        m = jnp.max(s, axis=1, keepdims=True)
        w = jnp.where(inside, jnp.exp(s - m), 0.0).astype(jnp.bfloat16)
        l = jnp.sum(w.astype(jnp.float32), axis=1, keepdims=True)
        u = jnp.dot(w, values, preferred_element_type=jnp.float32)
        for n, h in enumerate(heads):
            at = pl.ds(h * 64 + slot, 8, stride=8)
            e_scr[at, :] = u[n * 8 : n * 8 + 8, n * LANES : (n + 1) * LANES]
            m_scr[at, :] = jnp.broadcast_to(m[n * 8 : n * 8 + 8], (8, LANES))
            l_scr[at, :] = jnp.broadcast_to(l[n * 8 : n * 8 + 8], (8, LANES))


def gather_heads(e_scr, m_scr, l_scr, kv_heads, fresh):
    low = lax.broadcasted_iota(jnp.int32, (8, LANES), 1) < HD
    per_head = []
    for kv in range(kv_heads):
        for i in range(GROUP):
            even = pl.ds((kv * 8 + i) * 8, 8)
            odd = pl.ds((kv * 8 + 4 + i) * 8, 8)
            m_even, m_odd = m_scr[even, :], m_scr[odd, :]
            m = jnp.maximum(m_even, m_odd)
            if fresh is not None:
                q_scr, new_keys, new_values = fresh
                score = jnp.sum(q_scr[even, :] * new_keys[kv], axis=1, keepdims=True)
                m = jnp.maximum(m, score)
            by_even, by_odd = jnp.exp(m_even - m), jnp.exp(m_odd - m)
            l = l_scr[even, :] * by_even + l_scr[odd, :] * by_odd
            u = jnp.where(low, e_scr[even, :] * by_even, e_scr[odd, :] * by_odd)
            u = u + pltpu.roll(u, HD, 1)
            if fresh is not None:
                by_new = jnp.exp(score - m)
                l = l + by_new
                u = u + by_new * new_values[kv]
            per_head.append((u, m, l))
    blocks = []
    for j in range(len(per_head) // 2):
        blocks.append([jnp.where(low, a, b) for a, b in zip(per_head[2 * j], per_head[2 * j + 1])])
    return blocks


def pack_kernel(lengths_ref, split_ref, q_ref, out_ref):
    rows = q_ref.shape[0]
    slots = rows // 2
    picks = long_rows(lengths_ref, rows, slots)
    q = q_ref[...].astype(jnp.float32)
    row_id = lax.broadcasted_iota(jnp.int32, (rows, 1), 0)
    lane = lax.broadcasted_iota(jnp.int32, q.shape, 1)
    chosen, counts = jnp.zeros_like(q), jnp.zeros_like(q)
    for k in range(slots):
        row = jnp.sum(jnp.where(row_id == picks[k], q, 0.0), axis=0, keepdims=True)
        chosen = jnp.where(row_id == k, row, chosen)
        count = lengths_ref[picks[k]] - split_ref[picks[k]]
        counts = jnp.where(lane == 2 * k, (count // 32).astype(jnp.float32), counts)
        counts = jnp.where(lane == 2 * k + 1, (count % 32).astype(jnp.float32), counts)
    out_ref[...] = jnp.concatenate([chosen, counts], axis=0).astype(jnp.bfloat16)


def attend_kernel(
    split_ref, q_ref, far_ref, new_ref, home_ref, help_ref,
    home_out, help_out,
    k_buf, v_buf, hk_buf, hv_buf, q_scr, e_scr, m_scr, l_scr, hq_scr, he_scr, hm_scr, hl_scr, sems,
):
    rows, _, kv_heads = home_ref.shape[:3]
    slots = help_ref.shape[0]
    copies = []
    for r in range(rows):
        for c, buf in enumerate((k_buf, v_buf)):
            copy = pltpu.make_async_copy(home_ref.at[r, c], buf.at[r], sems.at[2 * r + c])
            copy.start()
            copies.append(copy)
    for s in range(slots):
        for c, buf in enumerate((hk_buf, hv_buf)):
            copy = pltpu.make_async_copy(help_ref.at[s, c], buf.at[s], sems.at[2 * (rows + s) + c])
            copy.start()
            copies.append(copy)

    place_queries(q_ref[...].astype(jnp.float32), q_scr, kv_heads)
    far = far_ref[...].astype(jnp.float32)
    place_queries(far[:8], hq_scr, kv_heads)
    counts = far[8:, :LANES]

    for r in range(rows):
        copies[2 * r].wait()
        copies[2 * r + 1].wait()
        one_slot(q_scr, k_buf.at[r], v_buf.at[r], e_scr, m_scr, l_scr, r, split_ref[r], kv_heads)
    low = lax.broadcasted_iota(jnp.int32, (8, LANES), 1) < HD
    new = new_ref[...].astype(jnp.float32)
    fresh = []
    for c in range(2):
        per_kv = []
        for kv in range(kv_heads):
            at = kv * HD // LANES * LANES
            width = min(LANES, kv_heads * HD)
            x = new[:, c, at : at + width]
            if width < LANES:
                x = jnp.concatenate([x, x], axis=1)
            swapped = pltpu.roll(x, HD, 1)
            per_kv.append(jnp.where(low, x, swapped) if kv % 2 == 0 else jnp.where(low, swapped, x))
        fresh.append(per_kv)
    home = gather_heads(e_scr, m_scr, l_scr, kv_heads, (q_scr, fresh[0], fresh[1]))
    for j, block in enumerate(home):
        for n in range(3):
            home_out[n, j] = block[n]

    for s in range(slots):
        copies[2 * (rows + s)].wait()
        copies[2 * (rows + s) + 1].wait()
        count = (counts[0, 2 * s] * 32.0 + counts[0, 2 * s + 1]).astype(jnp.int32)
        one_slot(hq_scr, hk_buf.at[s], hv_buf.at[s], he_scr, hm_scr, hl_scr, s, count, kv_heads)
    for j, (u, m, l) in enumerate(gather_heads(he_scr, hm_scr, hl_scr, kv_heads, None)):
        help_out[0, j] = (u / l)[:slots]
        help_out[1, j] = (m + jnp.log(l))[:slots]


def project_kernel(lengths_ref, home_ref, far_ref, w_ref, *outs):
    blocks, rows = home_ref.shape[1:3]
    slots = far_ref.shape[2]
    picks = long_rows(lengths_ref, rows, slots)
    row_id = lax.broadcasted_iota(jnp.int32, (rows, LANES), 0)
    mixes = []
    for j in range(blocks):
        far_o = jnp.zeros((rows, LANES), jnp.float32)
        far_m = jnp.full((rows, LANES), LOW, jnp.float32)
        for k in range(slots):
            at = row_id == picks[k]
            far_o = jnp.where(at, far_ref[0, j, pl.ds(k, 1), :], far_o)
            far_m = jnp.where(at, far_ref[1, j, pl.ds(k, 1), :], far_m)
        u, m, l = home_ref[0, j], home_ref[1, j], home_ref[2, j]
        top = jnp.maximum(m, far_m)
        near, far = jnp.exp(m - top), jnp.exp(far_m - top)
        mixes.append((u * near + far_o * far) / (l * near + far))
    mix = jnp.concatenate(mixes, axis=1).astype(jnp.bfloat16)
    if len(outs) == 1:
        outs[0][...] = jnp.dot(mix, w_ref[...], preferred_element_type=jnp.float32)
        return
    core = lax.axis_index("tp")
    width = outs[0].shape[1]
    for out, half in zip(outs, (core, 1 - core)):
        columns = pl.ds(pl.multiple_of(half * width, width), width)
        out[...] = jnp.dot(mix, w_ref[:, columns], preferred_element_type=jnp.float32)


def per_device(queries, new_kv, home_cache, help_cache, lengths, split_at, helper_req, out_weight):
    rows, _, kv_heads, context, lanes = home_cache.shape
    slots = help_cache.shape[0]
    groups, cores = lax.axis_size("grp"), lax.axis_size("tp")
    blocks = kv_heads * GROUP // 2
    partner = helper_req[0] // rows
    distance = jnp.bitwise_xor(lax.axis_index("grp"), partner)

    def exchange(x):
        if groups > MAX_BRANCHES:
            return lax.all_gather(x, "grp")[partner]

        def branch(k):
            pairs = [(g, g ^ k) for g in range(groups)]
            return lambda x: lax.ppermute(x, "grp", pairs)

        return lax.switch(distance - 1, [branch(k) for k in range(1, groups)], x)

    packed = pl.pallas_call(
        pack_kernel,
        out_shape=jax.ShapeDtypeStruct((2 * rows, queries.shape[1]), jnp.bfloat16),
        in_specs=[SMEM, SMEM, VMEM],
        out_specs=VMEM,
        name="pack",
    )(lengths, split_at, queries)
    far_queries = exchange(packed)

    small = pltpu.VMEM((kv_heads * 64, LANES), jnp.float32)
    home, partials = pl.pallas_call(
        attend_kernel,
        out_shape=(
            jax.ShapeDtypeStruct((3, blocks, rows, LANES), jnp.float32),
            jax.ShapeDtypeStruct((2, blocks, slots, LANES), jnp.float32),
        ),
        in_specs=[SMEM, VMEM, VMEM, VMEM, ANY, ANY],
        out_specs=(VMEM, VMEM),
        scratch_shapes=[
            pltpu.VMEM((rows, kv_heads, context, lanes), jnp.bfloat16),
            pltpu.VMEM((rows, kv_heads, context, lanes), jnp.bfloat16),
            pltpu.VMEM((slots, kv_heads, context, lanes), jnp.bfloat16),
            pltpu.VMEM((slots, kv_heads, context, lanes), jnp.bfloat16),
        ]
        + [small] * 8
        + [pltpu.SemaphoreType.DMA((2 * (rows + slots),))],
        compiler_params=pltpu.CompilerParams(vmem_limit_bytes=24 * MIB),
        name="attend",
    )(split_at, queries, far_queries, new_kv, home_cache, help_cache)

    far = exchange(partials)

    width = out_weight.shape[1] // cores
    pair = cores == 2
    shapes = [(rows, width)] * 2 if pair else [(rows, width * cores)]
    outs = pl.pallas_call(
        project_kernel,
        out_shape=[jax.ShapeDtypeStruct(s, jnp.float32) for s in shapes],
        in_specs=[SMEM, VMEM, VMEM, VMEM],
        out_specs=[VMEM] * len(shapes),
        compiler_params=pltpu.CompilerParams(vmem_limit_bytes=16 * MIB),
        name="project",
    )(lengths, home, far, out_weight)
    if pair:
        other = lax.ppermute(outs[1], "tp", [(0, 1), (1, 0)])
        return (outs[0] + other).astype(jnp.bfloat16)
    return lax.psum_scatter(outs[0], "tp", scatter_dimension=1, tiled=True).astype(jnp.bfloat16)


def solution(mesh):
    return jax.shard_map(
        per_device,
        mesh=mesh,
        in_specs=(
            P("grp", "tp"),
            P("grp", None, "tp"),
            P("grp", None, "tp", None, None),
            P("grp", None, "tp", None, None),
            P("grp"),
            P("grp"),
            P("grp"),
            P("tp", None),
        ),
        out_specs=P("grp", "tp"),
        check_vma=False,
    )
```

```python
import jax
import jax.numpy as jnp
from jax import lax
from jax.experimental import pallas as pl
from jax.experimental.pallas import tpu as pltpu
from jax.sharding import PartitionSpec as P

GROUP = 4
HD = 64
LANES = 2 * HD
CTX = 1024
LOW = -1e30
MIB = 1 << 20
MAX_BRANCHES = 32

VMEM = pl.BlockSpec(memory_space=pltpu.VMEM)
SMEM = pl.BlockSpec(memory_space=pltpu.SMEM)
ANY = pl.BlockSpec(memory_space=pl.ANY)


def long_rows(lengths, rows, slots):
    found = jnp.int32(0)
    picks = [jnp.int32(0)] * slots
    for r in range(rows):
        is_long = lengths[r] > CTX
        for k in range(slots):
            picks[k] = jnp.where(jnp.logical_and(is_long, found == k), jnp.int32(r), picks[k])
        found = found + is_long.astype(jnp.int32)
    return picks


def halves(x):
    low = lax.broadcasted_iota(jnp.int32, x.shape, x.ndim - 1) < HD
    swapped = pltpu.roll(x, HD, x.ndim - 1)
    return (
        (jnp.where(low, x, 0.0), jnp.where(low, 0.0, swapped)),
        (jnp.where(low, swapped, 0.0), jnp.where(low, 0.0, x)),
    )


def place_queries(x, q_scr, kv_heads):
    for j in range(kv_heads * GROUP // 2):
        block = halves(x[:, j * LANES : (j + 1) * LANES] * (HD**-0.5))
        for b in range(2):
            kv, i = divmod(2 * j + b, GROUP)
            for parity in range(2):
                q_scr[pl.ds((kv * 8 + parity * 4 + i) * 8, 8), :] = block[b][parity]


def attend(inside, cache_ref, q_scr, s_scr, p_scr, e_scr, m_scr, l_scr, kv_heads):
    pack = 2 if kv_heads % 2 == 0 else 1
    rows = 8 * pack
    items = kv_heads // pack

    def place(slot, h):
        return pl.ds(h * 64 + slot, 8, stride=8)

    def item_rows(slot, item):
        return pl.ds(pl.multiple_of((slot * items + item) * 16, 16), rows)

    def each(one):
        def stage(slot):
            for item in range(items):
                one(slot, item, range(item * pack, (item + 1) * pack))

        return stage

    def score(slot, item, heads):
        blocks = []
        for h in heads:
            part = q_scr[place(slot, h), :]
            zero = jnp.zeros_like(part)
            blocks.append(jnp.concatenate([part if o == h else zero for o in heads], axis=1))
        q = jnp.concatenate(blocks, axis=0).astype(jnp.bfloat16)
        keys = jnp.concatenate([cache_ref[2 * slot * kv_heads + h] for h in heads], axis=1)
        s = lax.dot_general(q, keys, (((1,), (1,)), ((), ())), preferred_element_type=jnp.float32)
        s_scr[item_rows(slot, item), :] = jnp.where(inside(slot, s.shape), s, LOW)

    def weigh(slot, item, heads):
        s = s_scr[item_rows(slot, item), :]
        m = jnp.max(s, axis=1, keepdims=True)
        p = jnp.exp(s - m).astype(jnp.bfloat16)
        p_scr[item_rows(slot, item), :] = p
        l = jnp.sum(p.astype(jnp.float32), axis=1, keepdims=True)
        for n, h in enumerate(heads):
            m_scr[place(slot, h), :] = jnp.broadcast_to(m[n * 8 : n * 8 + 8], (8, LANES))
            l_scr[place(slot, h), :] = jnp.broadcast_to(l[n * 8 : n * 8 + 8], (8, LANES))

    def mix(slot, item, heads):
        values = jnp.concatenate([cache_ref[(2 * slot + 1) * kv_heads + h] for h in heads], axis=1)
        u = jnp.dot(p_scr[item_rows(slot, item), :], values, preferred_element_type=jnp.float32)
        for n, h in enumerate(heads):
            e_scr[place(slot, h), :] = u[n * 8 : n * 8 + 8, n * LANES : (n + 1) * LANES]

    return each(score), each(weigh), each(mix)


def position(shape):
    parity = (lax.broadcasted_iota(jnp.int32, shape, 0) // 4) % 2
    return 2 * lax.broadcasted_iota(jnp.int32, shape, 1) + parity


def gather_heads(e_scr, m_scr, l_scr, kv_heads, fresh):
    low = lax.broadcasted_iota(jnp.int32, (8, LANES), 1) < HD
    heads = []
    for kv in range(kv_heads):
        for i in range(GROUP):
            even = pl.ds((kv * 8 + i) * 8, 8)
            odd = pl.ds((kv * 8 + 4 + i) * 8, 8)
            m_even, m_odd = m_scr[even, :], m_scr[odd, :]
            m = jnp.maximum(m_even, m_odd)
            if fresh is not None:
                q_scr, new_keys, new_values = fresh
                score = jnp.sum(q_scr[even, :] * new_keys[kv], axis=1, keepdims=True)
                m = jnp.maximum(m, score)
            by_even, by_odd = jnp.exp(m_even - m), jnp.exp(m_odd - m)
            l = l_scr[even, :] * by_even + l_scr[odd, :] * by_odd
            u = jnp.where(low, e_scr[even, :] * by_even, e_scr[odd, :] * by_odd)
            u = u + pltpu.roll(u, HD, 1)
            if fresh is not None:
                by_new = jnp.exp(score - m)
                l = l + by_new
                u = u + by_new * new_values[kv]
            heads.append((u, m, l))
    return heads


def pack_kernel(lengths_ref, split_ref, q_ref, out_ref, meta_ref):
    rows = q_ref.shape[0]
    slots = rows // 2
    picks = long_rows(lengths_ref, rows, slots)
    q = q_ref[...].astype(jnp.float32)
    row_id = lax.broadcasted_iota(jnp.int32, (rows, 1), 0)
    left = lax.broadcasted_iota(jnp.int32, q.shape, 1) < LANES
    meta_lane = lax.broadcasted_iota(jnp.int32, meta_ref.shape, 1)
    packed = jnp.zeros_like(q)
    meta = jnp.zeros(meta_ref.shape, jnp.int32)
    for k in range(slots):
        row = jnp.sum(jnp.where(row_id == picks[k], q, 0.0), axis=0, keepdims=True)
        packed = jnp.where(row_id == k, row, packed)
        count = lengths_ref[picks[k]] - split_ref[picks[k]]
        parts = jnp.where(left, (count // 32).astype(jnp.float32), (count % 32).astype(jnp.float32))
        packed = jnp.where(row_id == slots + k, parts, packed)
        meta = jnp.where(meta_lane == rows + k, picks[k], meta)
    for r in range(rows):
        meta = jnp.where(meta_lane == r, split_ref[r], meta)
    out_ref[...] = packed.astype(jnp.bfloat16)
    meta_ref[...] = meta


def home_kernel(
    meta_ref, q_ref, new_ref, home_ref, help_ref, out_ref, help_out,
    count_ref, cache, help_sem, sems, q_scr, s_scr, p_scr, e_scr, m_scr, l_scr,
):
    rows = q_ref.shape[0]
    kv_heads = home_ref.shape[0] // (2 * rows)
    at_once = 2

    def loop(body):
        def step(n, _):
            for i in range(at_once):
                body(n * at_once + i)
            return 0

        lax.fori_loop(0, rows // at_once, step, 0)

    def copy(slot, c):
        at = pl.ds((2 * slot + c) * kv_heads, kv_heads)
        return pltpu.make_async_copy(home_ref.at[at], cache.at[at], sems.at[2 * slot + c])

    for c in range(2):
        loop(lambda slot, c=c: copy(slot, c).start())
    help_copy = pltpu.make_async_copy(help_ref, help_out, help_sem)
    help_copy.start()

    meta = meta_ref[...]
    for r in range(rows):
        count_ref[r] = meta[0, r]
    place_queries(q_ref[...].astype(jnp.float32), q_scr, kv_heads)

    def inside(slot, shape):
        return position(shape) < count_ref[slot]

    score, weigh, mix = attend(inside, cache, q_scr, s_scr, p_scr, e_scr, m_scr, l_scr, kv_heads)

    def step(n, _):
        for i in range(at_once):
            copy(n * at_once + i, 0).wait()
        for i in range(at_once):
            score(n * at_once + i)
        return 0

    lax.fori_loop(0, rows // at_once, step, 0)
    loop(weigh)

    def step(n, _):
        for i in range(at_once):
            copy(n * at_once + i, 1).wait()
        for i in range(at_once):
            mix(n * at_once + i)
        return 0

    lax.fori_loop(0, rows // at_once, step, 0)

    low = lax.broadcasted_iota(jnp.int32, (8, LANES), 1) < HD
    new = new_ref[...].astype(jnp.float32)
    fresh = []
    for c in range(2):
        per_kv = []
        for kv in range(kv_heads):
            at = kv * HD // LANES * LANES
            width = min(LANES, kv_heads * HD)
            x = new[:, c, at : at + width]
            if width < LANES:
                x = jnp.concatenate([x, x], axis=1)
            swapped = pltpu.roll(x, HD, 1)
            per_kv.append(jnp.where(low, x, swapped) if kv % 2 == 0 else jnp.where(low, swapped, x))
        fresh.append(per_kv)
    heads = gather_heads(e_scr, m_scr, l_scr, kv_heads, (q_scr, *fresh))
    for j in range(len(heads) // 2):
        for n in range(3):
            out_ref[n, j] = jnp.where(low, heads[2 * j][n], heads[2 * j + 1][n])
    help_copy.wait()


def help_kernel(far_ref, cache_ref, out_ref, q_scr, s_scr, p_scr, e_scr, m_scr, l_scr):
    slots = out_ref.shape[0]
    kv_heads = cache_ref.shape[0] // (2 * slots)
    far = far_ref[...].astype(jnp.float32)
    counts = far[:, :LANES] * 32.0 + far[:, LANES : 2 * LANES]
    place_queries(far, q_scr, kv_heads)

    def inside(slot, shape):
        return position(shape).astype(jnp.float32) < counts[slots + slot : slots + slot + 1, :1]

    for stage in attend(inside, cache_ref, q_scr, s_scr, p_scr, e_scr, m_scr, l_scr, kv_heads):
        for slot in range(slots):
            stage(slot)
    heads = gather_heads(e_scr, m_scr, l_scr, kv_heads, None)
    lane = lax.broadcasted_iota(jnp.int32, (8, LANES), 1)
    logs = jnp.zeros((8, LANES), jnp.float32)
    for j in range(len(heads) // 2):
        mixed = jnp.where(lane < HD, *[u / l for u, _, l in heads[2 * j : 2 * j + 2]])
        out_ref[:, j * LANES : (j + 1) * LANES] = mixed[:slots]
        for h in (2 * j, 2 * j + 1):
            _, m, l = heads[h]
            logs = jnp.where(lane == h, m + jnp.log(l), logs)
    out_ref[:, len(heads) // 2 * LANES :] = logs[:slots]


def project_kernel(meta_ref, home_ref, far_ref, w_ref, *outs):
    blocks, rows = home_ref.shape[1:3]
    slots = far_ref.shape[0]
    meta = meta_ref[...]
    picks = [meta[0, rows + k] for k in range(slots)]
    row_id = lax.broadcasted_iota(jnp.int32, (rows, LANES), 0)
    low = lax.broadcasted_iota(jnp.int32, (slots, LANES), 1) < HD
    logs = far_ref[:, blocks * LANES :]
    mixes = []
    for j in range(blocks):
        block_o = far_ref[:, j * LANES : (j + 1) * LANES]
        block_m = jnp.where(low, logs[:, 2 * j : 2 * j + 1], logs[:, 2 * j + 1 : 2 * j + 2])
        far_o = jnp.zeros((rows, LANES), jnp.float32)
        far_m = jnp.full((rows, LANES), LOW, jnp.float32)
        for k in range(slots):
            at = row_id == picks[k]
            far_o = jnp.where(at, block_o[k : k + 1], far_o)
            far_m = jnp.where(at, block_m[k : k + 1], far_m)
        u, m, l = home_ref[0, j], home_ref[1, j], home_ref[2, j]
        top = jnp.maximum(m, far_m)
        near, far = jnp.exp(m - top), jnp.exp(far_m - top)
        mixes.append((u * near + far_o * far) / (l * near + far))
    mix = jnp.concatenate(mixes, axis=1).astype(jnp.bfloat16)
    core = lax.axis_index("tp")
    width = outs[0].shape[1]
    tile = min(512, width)
    for out, part in zip(outs, (core, 1 - core) if len(outs) == 2 else (0,)):

        def columns(n, _, out=out, part=part):
            source = pl.ds(pl.multiple_of(part * width + n * tile, tile), tile)
            target = pl.ds(pl.multiple_of(n * tile, tile), tile)
            out[:, target] = jnp.dot(mix, w_ref[:, source], preferred_element_type=jnp.float32)
            return 0

        lax.fori_loop(0, width // tile, columns, 0)


def scratch(slots, kv_heads, context):
    small = pltpu.VMEM((kv_heads * 64, LANES), jnp.float32)
    items = slots * max(kv_heads // 2, 1)
    return [
        small,
        pltpu.VMEM((items * 16, context), jnp.float32),
        pltpu.VMEM((items * 16, context), jnp.bfloat16),
        small,
        small,
        small,
    ]


def pack(lengths, split_at, queries):
    rows, width = queries.shape
    return pl.pallas_call(
        pack_kernel,
        out_shape=(
            jax.ShapeDtypeStruct((rows, width), jnp.bfloat16),
            jax.ShapeDtypeStruct((rows, LANES), jnp.int32),
        ),
        in_specs=[SMEM, SMEM, VMEM],
        out_specs=(VMEM, VMEM),
        name="pack",
    )(lengths, split_at, queries)


def attention(packed, meta, queries, new_kv, home_cache, help_cache, out_weight, exchange, cores):
    rows, _, kv_heads, context, lanes = home_cache.shape
    slots = help_cache.shape[0]
    blocks = kv_heads * GROUP // 2
    home_cache = home_cache.reshape(-1, context, lanes)
    help_cache = help_cache.reshape(-1, context, lanes)

    far_queries = exchange(packed)
    home, help_near = pl.pallas_call(
        home_kernel,
        out_shape=(
            jax.ShapeDtypeStruct((3, blocks, rows, LANES), jnp.float32),
            jax.ShapeDtypeStruct(help_cache.shape, jnp.bfloat16),
        ),
        in_specs=[VMEM, VMEM, VMEM, ANY, ANY],
        out_specs=(VMEM, VMEM),
        scratch_shapes=[
            pltpu.SMEM((rows,), jnp.int32),
            pltpu.VMEM(home_cache.shape, jnp.bfloat16),
            pltpu.SemaphoreType.DMA,
            pltpu.SemaphoreType.DMA((2 * rows,)),
        ]
        + scratch(rows, kv_heads, context),
        compiler_params=pltpu.CompilerParams(vmem_limit_bytes=32 * MIB),
        cost_estimate=pl.CostEstimate(
            flops=64 * home_cache.size, bytes_accessed=2 * (home_cache.size + help_cache.size), transcendentals=0
        ),
        name="home",
    )(meta, queries, new_kv, home_cache, help_cache)
    partials = pl.pallas_call(
        help_kernel,
        out_shape=jax.ShapeDtypeStruct((slots, (blocks + 1) * LANES), jnp.float32),
        in_specs=[VMEM, VMEM],
        out_specs=VMEM,
        scratch_shapes=scratch(slots, kv_heads, context),
        compiler_params=pltpu.CompilerParams(vmem_limit_bytes=16 * MIB),
        name="help",
    )(far_queries, help_near)
    far = exchange(partials)

    width = out_weight.shape[1] // cores
    shapes = [(rows, width)] * 2 if cores == 2 else [(rows, width * cores)]
    return tuple(
        pl.pallas_call(
            project_kernel,
            out_shape=[jax.ShapeDtypeStruct(shape, jnp.float32) for shape in shapes],
            in_specs=[VMEM] * 4,
            out_specs=[VMEM] * len(shapes),
            compiler_params=pltpu.CompilerParams(vmem_limit_bytes=16 * MIB),
            name="project",
        )(meta, home, far, out_weight)
    )


def per_device(queries, new_kv, home_cache, help_cache, lengths, split_at, helper_req, out_weight):
    groups, cores = lax.axis_size("grp"), lax.axis_size("tp")
    partner = (helper_req[0].astype(jnp.uint32) // queries.shape[0]).astype(jnp.int32)
    arrays = (*pack(lengths, split_at, queries), queries, new_kv, home_cache, help_cache, out_weight)
    if groups > MAX_BRANCHES:
        outs = attention(*arrays, lambda x: lax.all_gather(x, "grp")[partner], cores)
    else:

        def branch(k):
            pairs = [(g, g ^ k) for g in range(groups)]
            return lambda *xs: attention(*xs, lambda x: lax.ppermute(x, "grp", pairs), cores)

        distance = jnp.bitwise_xor(lax.axis_index("grp"), partner)
        outs = lax.switch(distance - 1, [branch(k) for k in range(1, groups)], *arrays)
    if cores == 2:
        other = lax.ppermute(outs[1], "tp", [(0, 1), (1, 0)])
        return (outs[0] + other).astype(jnp.bfloat16)
    return lax.psum_scatter(outs[0], "tp", scatter_dimension=1, tiled=True).astype(jnp.bfloat16)


def solution(mesh):
    return jax.shard_map(
        per_device,
        mesh=mesh,
        in_specs=(
            P("grp", "tp"),
            P("grp", None, "tp"),
            P("grp", None, "tp", None, None),
            P("grp", None, "tp", None, None),
            P("grp"),
            P("grp"),
            P("grp"),
            P("tp", None),
        ),
        out_specs=P("grp", "tp"),
        check_vma=False,
    )
```

```python
import functools

import jax
import jax.numpy as jnp
from jax import lax
from jax.experimental import pallas as pl
from jax.experimental.pallas import tpu as pltpu
from jax.sharding import PartitionSpec as P

GROUP = 4
HD = 64
LANES = 2 * HD
CTX = 1024
LOW = -1e30
AT_ONCE = 4
MIB = 1 << 20
MAX_BRANCHES = 32

VMEM = pl.BlockSpec(memory_space=pltpu.VMEM)
SMEM = pl.BlockSpec(memory_space=pltpu.SMEM)
ANY = pl.BlockSpec(memory_space=pl.ANY)


def long_rows(lengths, rows, slots):
    found = jnp.int32(0)
    picks = [jnp.int32(0)] * slots
    for r in range(rows):
        is_long = lengths[r] > CTX
        for k in range(slots):
            picks[k] = jnp.where(jnp.logical_and(is_long, found == k), jnp.int32(r), picks[k])
        found = found + is_long.astype(jnp.int32)
    return picks


def halves(x):
    low = lax.broadcasted_iota(jnp.int32, x.shape, x.ndim - 1) < HD
    swapped = pltpu.roll(x, HD, x.ndim - 1)
    return (
        (jnp.where(low, x, 0.0), jnp.where(low, 0.0, swapped)),
        (jnp.where(low, swapped, 0.0), jnp.where(low, 0.0, x)),
    )


def place_queries(x, q_scr, kv_heads):
    for j in range(kv_heads * GROUP // 2):
        block = halves(x[:, j * LANES : (j + 1) * LANES] * (HD**-0.5))
        for b in range(2):
            kv, i = divmod(2 * j + b, GROUP)
            for parity in range(2):
                q_scr[pl.ds((kv * 8 + parity * 4 + i) * 8, 8), :] = block[b][parity]


def attend(inside, block, q_scr, s_scr, p_scr, e_scr, m_scr, l_scr, kv_heads):
    pack = 2 if kv_heads % 2 == 0 else 1
    rows = 8 * pack
    items = kv_heads // pack

    def place(slot, h):
        return pl.ds(h * 64 + slot, 8, stride=8)

    def item_rows(slot, item):
        return pl.ds(pl.multiple_of((slot * items + item) * 16, 16), rows)

    def each(one):
        def stage(slot):
            for item in range(items):
                one(slot, item, range(item * pack, (item + 1) * pack))

        return stage

    def score(slot, item, heads):
        blocks = []
        for h in heads:
            part = q_scr[place(slot, h), :]
            zero = jnp.zeros_like(part)
            blocks.append(jnp.concatenate([part if o == h else zero for o in heads], axis=1))
        q = jnp.concatenate(blocks, axis=0).astype(jnp.bfloat16)
        keys = jnp.concatenate([block(slot, 0, h) for h in heads], axis=1)
        s = lax.dot_general(q, keys, (((1,), (1,)), ((), ())), preferred_element_type=jnp.float32)
        s_scr[item_rows(slot, item), :] = jnp.where(inside(slot, s.shape), s, LOW)

    def weigh(slot, item, heads):
        s = s_scr[item_rows(slot, item), :]
        m = jnp.max(s, axis=1, keepdims=True)
        p = jnp.exp(s - m).astype(jnp.bfloat16)
        p_scr[item_rows(slot, item), :] = p
        l = jnp.sum(p.astype(jnp.float32), axis=1, keepdims=True)
        for n, h in enumerate(heads):
            m_scr[place(slot, h), :] = jnp.broadcast_to(m[n * 8 : n * 8 + 8], (8, LANES))
            l_scr[place(slot, h), :] = jnp.broadcast_to(l[n * 8 : n * 8 + 8], (8, LANES))

    def mix(slot, item, heads):
        values = jnp.concatenate([block(slot, 1, h) for h in heads], axis=1)
        u = jnp.dot(p_scr[item_rows(slot, item), :], values, preferred_element_type=jnp.float32)
        for n, h in enumerate(heads):
            e_scr[place(slot, h), :] = u[n * 8 : n * 8 + 8, n * LANES : (n + 1) * LANES]

    return each(score), each(weigh), each(mix)


def position(shape):
    parity = (lax.broadcasted_iota(jnp.int32, shape, 0) // 4) % 2
    return 2 * lax.broadcasted_iota(jnp.int32, shape, 1) + parity


def gather_heads(e_scr, m_scr, l_scr, kv_heads, fresh):
    low = lax.broadcasted_iota(jnp.int32, (8, LANES), 1) < HD
    heads = []
    for kv in range(kv_heads):
        for i in range(GROUP):
            even = pl.ds((kv * 8 + i) * 8, 8)
            odd = pl.ds((kv * 8 + 4 + i) * 8, 8)
            m_even, m_odd = m_scr[even, :], m_scr[odd, :]
            m = jnp.maximum(m_even, m_odd)
            if fresh is not None:
                q_scr, new_keys, new_values = fresh
                score = jnp.sum(q_scr[even, :] * new_keys[kv], axis=1, keepdims=True)
                m = jnp.maximum(m, score)
            by_even, by_odd = jnp.exp(m_even - m), jnp.exp(m_odd - m)
            l = l_scr[even, :] * by_even + l_scr[odd, :] * by_odd
            u = jnp.where(low, e_scr[even, :] * by_even, e_scr[odd, :] * by_odd)
            u = u + pltpu.roll(u, HD, 1)
            if fresh is not None:
                by_new = jnp.exp(score - m)
                l = l + by_new
                u = u + by_new * new_values[kv]
            heads.append((u, m, l))
    return heads


def attend_home(first, last, home_ref, cache, sems, count_ref, scratches, kv_heads):
    def slots_of(n):
        return [AT_ONCE * n + i for i in range(AT_ONCE)]

    def loop(body):
        def step(n, _):
            for slot in slots_of(n):
                body(slot)
            return 0

        lax.fori_loop(first, last, step, 0)

    def copy(slot, c):
        at = pl.ds((2 * slot + c) * kv_heads, kv_heads)
        return pltpu.make_async_copy(home_ref.at[at], cache.at[at], sems.at[2 * slot + c])

    def inside(slot, shape):
        return position(shape) < count_ref[slot]

    score, weigh, mix = attend(
        inside, lambda slot, c, h: cache[(2 * slot + c) * kv_heads + h], *scratches, kv_heads
    )

    def start():
        for c in range(2):
            loop(lambda slot, c=c: copy(slot, c).start())

    def step(c, stage):
        def body(n, _):
            for slot in slots_of(n):
                copy(slot, c).wait()
            for slot in slots_of(n):
                stage(slot)
            return 0

        lax.fori_loop(first, last, body, 0)

    def run():
        step(0, score)
        loop(weigh)
        step(1, mix)

    return start, run


def hops(group):
    return (group >> 2) + ((group >> 1) & 1) + (group & 1)


def pack_kernel(
    lengths_ref, split_ref, helper_ref, q_ref, home_ref,
    out_ref, meta_ref, e_ref, m_ref, l_ref,
    count_ref, cache, sems, q_scr, s_scr, p_scr, *, groups,
):
    rows = q_ref.shape[0]
    kv_heads = home_ref.shape[0] // (2 * rows)
    slots = rows // 2
    me = lax.axis_index("grp")
    partner = helper_ref[0] // rows
    done = jnp.int32(0)
    if groups == 16:
        done = (hops(partner) - hops(me) > 2).astype(jnp.int32)
    scratches = (q_scr, s_scr, p_scr, e_ref, m_ref, l_ref)
    start, run = attend_home(0, done, home_ref, cache, sems, count_ref, scratches, kv_heads)

    @pl.when(done > 0)
    def _():
        start()

    picks = long_rows(lengths_ref, rows, slots)
    q = q_ref[...].astype(jnp.float32)
    row_id = lax.broadcasted_iota(jnp.int32, (rows, 1), 0)
    left = lax.broadcasted_iota(jnp.int32, q.shape, 1) < LANES
    meta_lane = lax.broadcasted_iota(jnp.int32, meta_ref.shape, 1)
    packed = jnp.zeros_like(q)
    meta = jnp.zeros(meta_ref.shape, jnp.int32)
    for k in range(slots):
        row = jnp.sum(jnp.where(row_id == picks[k], q, 0.0), axis=0, keepdims=True)
        packed = jnp.where(row_id == k, row, packed)
        count = lengths_ref[picks[k]] - split_ref[picks[k]]
        parts = jnp.where(left, (count // 32).astype(jnp.float32), (count % 32).astype(jnp.float32))
        packed = jnp.where(row_id == slots + k, parts, packed)
        meta = jnp.where(meta_lane == 1 + rows + k, picks[k], meta)
    for r in range(rows):
        meta = jnp.where(meta_lane == 1 + r, split_ref[r], meta)
    out_ref[...] = packed.astype(jnp.bfloat16)
    meta_ref[...] = jnp.where(meta_lane == 1 + rows + slots, done, meta)

    @pl.when(done > 0)
    def _():
        for r in range(rows):
            count_ref[r] = split_ref[r]
        place_queries(q, q_scr, kv_heads)
        run()


def home_kernel(
    meta_ref, q_ref, new_ref, e_ref, m_ref, l_ref, home_ref, out_ref,
    count_ref, cache, sems, q_scr, s_scr, p_scr, e_scr, m_scr, l_scr,
):
    rows = q_ref.shape[0]
    kv_heads = home_ref.shape[0] // (2 * rows)
    meta = meta_ref[...]
    done = meta[0, 1 + rows + rows // 2]
    scratches = (q_scr, s_scr, p_scr, e_scr, m_scr, l_scr)
    start, run = attend_home(done, rows // AT_ONCE, home_ref, cache, sems, count_ref, scratches, kv_heads)
    start()

    for r in range(rows):
        count_ref[r] = meta[0, 1 + r]
    place_queries(q_ref[...].astype(jnp.float32), q_scr, kv_heads)
    for scr, ref in ((e_scr, e_ref), (m_scr, m_ref), (l_scr, l_ref)):
        scr[...] = ref[...]
    run()

    low = lax.broadcasted_iota(jnp.int32, (8, LANES), 1) < HD
    new = new_ref[...].astype(jnp.float32)
    fresh = []
    for c in range(2):
        per_kv = []
        for kv in range(kv_heads):
            at = kv * HD // LANES * LANES
            width = min(LANES, kv_heads * HD)
            x = new[:, c, at : at + width]
            if width < LANES:
                x = jnp.concatenate([x, x], axis=1)
            swapped = pltpu.roll(x, HD, 1)
            per_kv.append(jnp.where(low, x, swapped) if kv % 2 == 0 else jnp.where(low, swapped, x))
        fresh.append(per_kv)
    heads = gather_heads(e_scr, m_scr, l_scr, kv_heads, (q_scr, *fresh))
    for j in range(len(heads) // 2):
        for n in range(3):
            out_ref[n, j] = jnp.where(low, heads[2 * j][n], heads[2 * j + 1][n])


def help_kernel(far_ref, after_ref, cache_ref, out_ref, q_scr, s_scr, p_scr, e_scr, m_scr, l_scr):
    slots = out_ref.shape[0]
    kv_heads = cache_ref.shape[2]
    far = far_ref[...].astype(jnp.float32)
    counts = far[:, :LANES] * 32.0 + far[:, LANES : 2 * LANES]
    place_queries(far, q_scr, kv_heads)

    def inside(slot, shape):
        return position(shape).astype(jnp.float32) < counts[slots + slot : slots + slot + 1, :1]

    for stage in attend(inside, lambda slot, c, h: cache_ref[slot, c, h], q_scr, s_scr, p_scr, e_scr, m_scr, l_scr, kv_heads):
        for slot in range(slots):
            stage(slot)
    heads = gather_heads(e_scr, m_scr, l_scr, kv_heads, None)
    lane = lax.broadcasted_iota(jnp.int32, (8, LANES), 1)
    logs = jnp.zeros((8, LANES), jnp.float32)
    for j in range(len(heads) // 2):
        mixed = jnp.where(lane < HD, *[u / l for u, _, l in heads[2 * j : 2 * j + 2]])
        out_ref[:, j * LANES : (j + 1) * LANES] = mixed[:slots]
        for h in (2 * j, 2 * j + 1):
            _, m, l = heads[h]
            logs = jnp.where(lane == h, m + jnp.log(l), logs)
    out_ref[:, len(heads) // 2 * LANES :] = logs[:slots]


def project_kernel(meta_ref, home_ref, far_ref, w_ref, out_ref, *mix_ref):
    blocks, rows = home_ref.shape[1:3]
    slots = far_ref.shape[0]
    meta = meta_ref[...]
    picks = [meta[0, 1 + rows + k] for k in range(slots)]
    row_id = lax.broadcasted_iota(jnp.int32, (rows, LANES), 0)
    low = lax.broadcasted_iota(jnp.int32, (slots, LANES), 1) < HD
    logs = far_ref[:, blocks * LANES :]
    mixes = []
    for j in range(blocks):
        block_o = far_ref[:, j * LANES : (j + 1) * LANES]
        block_m = jnp.where(low, logs[:, 2 * j : 2 * j + 1], logs[:, 2 * j + 1 : 2 * j + 2])
        far_o = jnp.zeros((rows, LANES), jnp.float32)
        far_m = jnp.full((rows, LANES), LOW, jnp.float32)
        for k in range(slots):
            at = row_id == picks[k]
            far_o = jnp.where(at, block_o[k : k + 1], far_o)
            far_m = jnp.where(at, block_m[k : k + 1], far_m)
        u, m, l = home_ref[0, j], home_ref[1, j], home_ref[2, j]
        top = jnp.maximum(m, far_m)
        near, far = jnp.exp(m - top), jnp.exp(far_m - top)
        mixes.append((u * near + far_o * far) / (l * near + far))
    mix = jnp.concatenate(mixes, axis=1).astype(jnp.bfloat16)
    for ref in mix_ref:
        ref[...] = mix
    project(mix, w_ref, out_ref, 1 - lax.axis_index("tp") if mix_ref else 0)


def project(mix, w_ref, out_ref, part):
    width = out_ref.shape[1]
    tile = min(512, width)

    def columns(n, _):
        source = pl.ds(pl.multiple_of(part * width + n * tile, tile), tile)
        target = pl.ds(pl.multiple_of(n * tile, tile), tile)
        out_ref[:, target] = jnp.dot(mix, w_ref[:, source], preferred_element_type=jnp.float32)
        return 0

    lax.fori_loop(0, width // tile, columns, 0)


def own_kernel(mix_ref, w_ref, out_ref):
    project(mix_ref[...], w_ref, out_ref, lax.axis_index("tp"))


def scratch(slots, kv_heads, context):
    small = pltpu.VMEM((kv_heads * 64, LANES), jnp.float32)
    items = slots * max(kv_heads // 2, 1)
    return [
        small,
        pltpu.VMEM((items * 16, context), jnp.float32),
        pltpu.VMEM((items * 16, context), jnp.bfloat16),
        small,
        small,
        small,
    ]


def home_scratch(rows, cache):
    return [
        pltpu.SMEM((rows,), jnp.int32),
        pltpu.VMEM(cache.shape, jnp.bfloat16),
    ]


def pack(lengths, split_at, helper_req, queries, home_cache, groups):
    rows, width = queries.shape
    _, _, kv_heads, context, lanes = home_cache.shape
    home_cache = home_cache.reshape(-1, context, lanes)
    small = jax.ShapeDtypeStruct((kv_heads * 64, LANES), jnp.float32)
    return pl.pallas_call(
        functools.partial(pack_kernel, groups=groups),
        out_shape=(
            jax.ShapeDtypeStruct((rows, width), jnp.bfloat16),
            jax.ShapeDtypeStruct((rows, LANES), jnp.int32),
            small,
            small,
            small,
        ),
        in_specs=[SMEM, SMEM, SMEM, VMEM, ANY],
        out_specs=(VMEM,) * 5,
        scratch_shapes=home_scratch(rows, home_cache)
        + [pltpu.SemaphoreType.DMA((2 * rows,))]
        + scratch(rows, kv_heads, context)[:3],
        compiler_params=pltpu.CompilerParams(vmem_limit_bytes=60 * MIB),
        name="pack",
    )(lengths, split_at, helper_req, queries, home_cache)


def attention(packed, meta, early, queries, new_kv, home_cache, help_cache, out_weight, exchange, cores):
    rows, _, kv_heads, context, lanes = home_cache.shape
    slots = help_cache.shape[0]
    blocks = kv_heads * GROUP // 2
    home_cache = home_cache.reshape(-1, context, lanes)

    far_queries = exchange(packed)
    home = pl.pallas_call(
        home_kernel,
        out_shape=jax.ShapeDtypeStruct((3, blocks, rows, LANES), jnp.float32),
        in_specs=[VMEM] * 6 + [ANY],
        out_specs=VMEM,
        scratch_shapes=home_scratch(rows, home_cache)
        + [pltpu.SemaphoreType.DMA((2 * rows,))]
        + scratch(rows, kv_heads, context),
        compiler_params=pltpu.CompilerParams(vmem_limit_bytes=32 * MIB),
        cost_estimate=pl.CostEstimate(
            flops=64 * home_cache.size, bytes_accessed=2 * home_cache.size, transcendentals=0
        ),
        name="home",
    )(meta, queries, new_kv, *early, home_cache)
    partials = pl.pallas_call(
        help_kernel,
        out_shape=jax.ShapeDtypeStruct((slots, (blocks + 1) * LANES), jnp.float32),
        in_specs=[VMEM, ANY, VMEM],
        out_specs=VMEM,
        scratch_shapes=scratch(slots, kv_heads, context),
        compiler_params=pltpu.CompilerParams(vmem_limit_bytes=16 * MIB),
        name="help",
    )(far_queries, home, help_cache)
    far = exchange(partials)

    pair = cores == 2
    width = out_weight.shape[1] // (cores if pair else 1)
    partial = jax.ShapeDtypeStruct((rows, width), jnp.float32)
    mix = jax.ShapeDtypeStruct((rows, blocks * LANES), jnp.bfloat16)
    projected = pl.pallas_call(
        project_kernel,
        out_shape=(partial, mix) if pair else (partial,),
        in_specs=[VMEM] * 4,
        out_specs=(VMEM, VMEM) if pair else (VMEM,),
        compiler_params=pltpu.CompilerParams(vmem_limit_bytes=16 * MIB),
        name="project",
    )(meta, home, far, out_weight)
    if not pair:
        return projected[0]
    other = lax.ppermute(projected[0], "tp", [(0, 1), (1, 0)])
    own = pl.pallas_call(
        own_kernel,
        out_shape=partial,
        in_specs=[VMEM, VMEM],
        out_specs=VMEM,
        compiler_params=pltpu.CompilerParams(vmem_limit_bytes=16 * MIB),
        cost_estimate=pl.CostEstimate(
            flops=2 * rows * out_weight.size, bytes_accessed=out_weight.size, transcendentals=0
        ),
        name="own",
    )(projected[1], out_weight)
    return (own + other).astype(jnp.bfloat16)


def per_device(queries, new_kv, home_cache, help_cache, lengths, split_at, helper_req, out_weight):
    groups, cores = lax.axis_size("grp"), lax.axis_size("tp")
    partner = helper_req[0].astype(jnp.uint32) // queries.shape[0]
    distance = jnp.bitwise_xor(lax.axis_index("grp").astype(jnp.uint32), partner).astype(jnp.int32)
    packed, meta, *early = pack(lengths, split_at, helper_req, queries, home_cache, groups)
    arrays = (packed, meta, early, queries, new_kv, home_cache, help_cache, out_weight)
    if groups > MAX_BRANCHES:
        out = attention(*arrays, lambda x: lax.all_gather(x, "grp")[partner], cores)
    else:

        def at_distance(k):
            pairs = [(g, g ^ k) for g in range(groups)]
            return lambda *xs: attention(*xs, lambda x: lax.ppermute(x, "grp", pairs), cores)

        branches = [at_distance(k) for k in reversed(range(1, groups))]
        out = lax.switch(groups - 1 - distance, branches, *arrays)
    if cores == 2:
        return out
    return lax.psum_scatter(out, "tp", scatter_dimension=1, tiled=True).astype(jnp.bfloat16)


def solution(mesh):
    return jax.shard_map(
        per_device,
        mesh=mesh,
        in_specs=(
            P("grp", "tp"),
            P("grp", None, "tp"),
            P("grp", None, "tp", None, None),
            P("grp", None, "tp", None, None),
            P("grp"),
            P("grp"),
            P("grp"),
            P("tp", None),
        ),
        out_specs=P("grp", "tp"),
        check_vma=False,
    )
```

```python
import functools

import jax
import jax.numpy as jnp
from jax import lax
from jax.experimental import pallas as pl
from jax.experimental.pallas import tpu as pltpu
from jax.sharding import PartitionSpec as P

GROUP = 4
HD = 64
LANES = 2 * HD
CTX = 1024
LOW = -1e30
AT_ONCE = 4
STEP = 64
MIB = 1 << 20
MAX_BRANCHES = 32

VMEM = pl.BlockSpec(memory_space=pltpu.VMEM)
SMEM = pl.BlockSpec(memory_space=pltpu.SMEM)
ANY = pl.BlockSpec(memory_space=pl.ANY)


def long_rows(lengths, rows, slots):
    found = jnp.int32(0)
    picks = [jnp.int32(0)] * slots
    for r in range(rows):
        is_long = lengths[r] > CTX
        for k in range(slots):
            picks[k] = jnp.where(jnp.logical_and(is_long, found == k), jnp.int32(r), picks[k])
        found = found + is_long.astype(jnp.int32)
    return picks


def halves(x):
    low = lax.broadcasted_iota(jnp.int32, x.shape, x.ndim - 1) < HD
    swapped = pltpu.roll(x, HD, x.ndim - 1)
    return (
        (jnp.where(low, x, 0.0), jnp.where(low, 0.0, swapped)),
        (jnp.where(low, swapped, 0.0), jnp.where(low, 0.0, x)),
    )


def place_queries(x, q_scr, kv_heads):
    for j in range(kv_heads * GROUP // 2):
        block = halves(x[:, j * LANES : (j + 1) * LANES] * (HD**-0.5))
        for b in range(2):
            kv, i = divmod(2 * j + b, GROUP)
            for parity in range(2):
                q_scr[pl.ds((kv * 8 + parity * 4 + i) * 8, 8), :] = block[b][parity]


def attend(inside, block, q_scr, s_scr, p_scr, e_scr, m_scr, l_scr, kv_heads):
    pack = 2 if kv_heads % 2 == 0 else 1
    rows = 8 * pack
    items = kv_heads // pack

    def place(slot, h):
        return pl.ds(h * 64 + slot, 8, stride=8)

    def item_rows(slot, item):
        return pl.ds(pl.multiple_of((slot * items + item) * 16, 16), rows)

    def each(one):
        def stage(slot):
            for item in range(items):
                one(slot, item, range(item * pack, (item + 1) * pack))

        return stage

    def score(slot, item, heads):
        blocks = []
        for h in heads:
            part = q_scr[place(slot, h), :]
            zero = jnp.zeros_like(part)
            blocks.append(jnp.concatenate([part if o == h else zero for o in heads], axis=1))
        q = jnp.concatenate(blocks, axis=0).astype(jnp.bfloat16)
        keys = jnp.concatenate([block(slot, 0, h) for h in heads], axis=1)
        s = lax.dot_general(q, keys, (((1,), (1,)), ((), ())), preferred_element_type=jnp.float32)
        s_scr[item_rows(slot, item), :] = jnp.where(inside(slot, s.shape), s, LOW)

    def weigh(slot, item, heads):
        s = s_scr[item_rows(slot, item), :]
        m = jnp.max(s, axis=1, keepdims=True)
        p = jnp.exp(s - m).astype(jnp.bfloat16)
        p_scr[item_rows(slot, item), :] = p
        l = jnp.sum(p.astype(jnp.float32), axis=1, keepdims=True)
        for n, h in enumerate(heads):
            m_scr[place(slot, h), :] = jnp.broadcast_to(m[n * 8 : n * 8 + 8], (8, LANES))
            l_scr[place(slot, h), :] = jnp.broadcast_to(l[n * 8 : n * 8 + 8], (8, LANES))

    def mix(slot, item, heads):
        values = jnp.concatenate([block(slot, 1, h) for h in heads], axis=1)
        u = jnp.dot(p_scr[item_rows(slot, item), :], values, preferred_element_type=jnp.float32)
        for n, h in enumerate(heads):
            e_scr[place(slot, h), :] = u[n * 8 : n * 8 + 8, n * LANES : (n + 1) * LANES]

    return each(score), each(weigh), each(mix)


def position(shape):
    parity = (lax.broadcasted_iota(jnp.int32, shape, 0) // 4) % 2
    return 2 * lax.broadcasted_iota(jnp.int32, shape, 1) + parity


def gather_heads(e_scr, m_scr, l_scr, kv_heads, fresh):
    low = lax.broadcasted_iota(jnp.int32, (8, LANES), 1) < HD
    heads = []
    for kv in range(kv_heads):
        for i in range(GROUP):
            even = pl.ds((kv * 8 + i) * 8, 8)
            odd = pl.ds((kv * 8 + 4 + i) * 8, 8)
            m_even, m_odd = m_scr[even, :], m_scr[odd, :]
            m = jnp.maximum(m_even, m_odd)
            if fresh is not None:
                q_scr, new_keys, new_values = fresh
                score = jnp.sum(q_scr[even, :] * new_keys[kv], axis=1, keepdims=True)
                m = jnp.maximum(m, score)
            by_even, by_odd = jnp.exp(m_even - m), jnp.exp(m_odd - m)
            l = l_scr[even, :] * by_even + l_scr[odd, :] * by_odd
            u = jnp.where(low, e_scr[even, :] * by_even, e_scr[odd, :] * by_odd)
            u = u + pltpu.roll(u, HD, 1)
            if fresh is not None:
                by_new = jnp.exp(score - m)
                l = l + by_new
                u = u + by_new * new_values[kv]
            heads.append((u, m, l))
    return heads


def attend_home(first, last, home_ref, cache, sems, count_ref, scratches, kv_heads):
    def slots_of(n):
        return [AT_ONCE * n + i for i in range(AT_ONCE)]

    def loop(body):
        def step(n, _):
            for slot in slots_of(n):
                body(slot)
            return 0

        lax.fori_loop(first, last, step, 0)

    def steps(slot):
        return (count_ref[slot] + (2 * STEP - 1)) >> STEP.bit_length()

    def copy(slot, c):
        at = pl.ds((2 * slot + c) * kv_heads, kv_heads)
        filled = pl.ds(0, pl.multiple_of(steps(slot) * STEP, STEP))
        return pltpu.make_async_copy(home_ref.at[at, filled], cache.at[at, filled], sems.at[2 * slot + c])

    def clear_rest(slot, _):
        def clear(n, _):
            at = pl.ds(pl.multiple_of(n * STEP, STEP), STEP)
            for h in range(kv_heads):
                cache[(2 * slot + 1) * kv_heads + h, at, :] = jnp.zeros((STEP, LANES), jnp.bfloat16)
            return 0

        return lax.fori_loop(steps(slot), cache.shape[1] // STEP, clear, 0)

    def inside(slot, shape):
        return position(shape) < count_ref[slot]

    score, weigh, mix = attend(
        inside, lambda slot, c, h: cache[(2 * slot + c) * kv_heads + h], *scratches, kv_heads
    )

    def begin(c):
        def one(slot, _):
            copy(slot, c).start()
            return 0

        lax.fori_loop(AT_ONCE * first, AT_ONCE * last, one, 0)

    def start():
        begin(0)
        begin(1)
        lax.fori_loop(AT_ONCE * first, AT_ONCE * last, clear_rest, 0)

    def step(c, stage):
        def body(n, _):
            for slot in slots_of(n):
                copy(slot, c).wait()
            for slot in slots_of(n):
                stage(slot)
            return 0

        lax.fori_loop(first, last, body, 0)

    def run():
        step(0, score)
        loop(weigh)
        step(1, mix)

    return start, run


def hops(group):
    return (group >> 2) + ((group >> 1) & 1) + (group & 1)


def pack_kernel(
    lengths_in, split_in, helper_in, q_in, home_ref,
    out_ref, meta_ref, e_ref, m_ref, l_ref,
    lengths_ref, split_ref, helper_ref, q_ref, in_sems, cache, sems, q_scr, s_scr, p_scr, *, groups,
):
    arrays = ((helper_in, helper_ref), (split_in, split_ref), (lengths_in, lengths_ref), (q_in, q_ref))
    copies = [pltpu.make_async_copy(*pair, in_sems.at[n]) for n, pair in enumerate(arrays)]
    for copy in copies:
        copy.start()
    for copy in copies:
        copy.wait()
    rows = q_ref.shape[0]
    kv_heads = home_ref.shape[0] // (2 * rows)
    slots = rows // 2
    me = lax.axis_index("grp")
    partner = helper_ref[0] // rows
    done = jnp.int32(0)
    if groups == 16:
        done = (hops(partner) - hops(me) > 2).astype(jnp.int32)
    scratches = (q_scr, s_scr, p_scr, e_ref, m_ref, l_ref)
    start, run = attend_home(0, done, home_ref, cache, sems, split_ref, scratches, kv_heads)

    @pl.when(done > 0)
    def _():
        start()

    picks = long_rows(lengths_ref, rows, slots)
    q = q_ref[...].astype(jnp.float32)
    row_id = lax.broadcasted_iota(jnp.int32, (rows, 1), 0)
    left = lax.broadcasted_iota(jnp.int32, q.shape, 1) < LANES
    meta_lane = lax.broadcasted_iota(jnp.int32, meta_ref.shape, 1)
    packed = jnp.zeros_like(q)
    meta = jnp.zeros(meta_ref.shape, jnp.int32)
    for k in range(slots):
        row = jnp.sum(jnp.where(row_id == picks[k], q, 0.0), axis=0, keepdims=True)
        packed = jnp.where(row_id == k, row, packed)
        count = lengths_ref[picks[k]] - split_ref[picks[k]]
        parts = jnp.where(left, (count // 32).astype(jnp.float32), (count % 32).astype(jnp.float32))
        packed = jnp.where(row_id == slots + k, parts, packed)
        meta = jnp.where(meta_lane == 1 + rows + k, picks[k], meta)
    for r in range(rows):
        meta = jnp.where(meta_lane == 1 + r, split_ref[r], meta)
    out_ref[...] = packed.astype(jnp.bfloat16)
    meta_ref[...] = jnp.where(meta_lane == 1 + rows + slots, done, meta)

    @pl.when(done > 0)
    def _():
        place_queries(q, q_scr, kv_heads)
        run()


def home_kernel(
    meta_ref, q_ref, e_ref, m_ref, l_ref, home_ref, e_out, m_out, l_out, count_ref, cache, sems, q_scr, s_scr, p_scr
):
    rows = q_ref.shape[0]
    kv_heads = home_ref.shape[0] // (2 * rows)
    meta = meta_ref[...]
    done = meta[0, 1 + rows + rows // 2]
    scratches = (q_scr, s_scr, p_scr, e_out, m_out, l_out)
    start, run = attend_home(done, rows // AT_ONCE, home_ref, cache, sems, count_ref, scratches, kv_heads)
    for r in range(rows):
        count_ref[r] = meta[0, 1 + r]
    start()
    place_queries(q_ref[...].astype(jnp.float32), q_scr, kv_heads)

    @pl.when(done > 0)
    def _():
        for out, ref in ((e_out, e_ref), (m_out, m_ref), (l_out, l_ref)):
            out[...] = ref[...]

    run()


def finish_kernel(q_ref, new_ref, e_ref, m_ref, l_ref, after_ref, out_ref, q_scr):
    kv_heads = q_ref.shape[1] // (GROUP * HD)
    place_queries(q_ref[...].astype(jnp.float32), q_scr, kv_heads)
    low = lax.broadcasted_iota(jnp.int32, (8, LANES), 1) < HD
    new = new_ref[...].astype(jnp.float32)
    fresh = []
    for c in range(2):
        per_kv = []
        for kv in range(kv_heads):
            at = kv * HD // LANES * LANES
            width = min(LANES, kv_heads * HD)
            x = new[:, c, at : at + width]
            if width < LANES:
                x = jnp.concatenate([x, x], axis=1)
            swapped = pltpu.roll(x, HD, 1)
            per_kv.append(jnp.where(low, x, swapped) if kv % 2 == 0 else jnp.where(low, swapped, x))
        fresh.append(per_kv)
    heads = gather_heads(e_ref, m_ref, l_ref, kv_heads, (q_scr, *fresh))
    for j in range(len(heads) // 2):
        for n in range(3):
            out_ref[n, j] = jnp.where(low, heads[2 * j][n], heads[2 * j + 1][n])


def help_kernel(far_ref, after_ref, cache_ref, out_ref, q_scr, s_scr, p_scr, e_scr, m_scr, l_scr):
    slots = out_ref.shape[0]
    kv_heads = cache_ref.shape[2]
    far = far_ref[...].astype(jnp.float32)
    counts = far[:, :LANES] * 32.0 + far[:, LANES : 2 * LANES]
    place_queries(far, q_scr, kv_heads)

    def inside(slot, shape):
        return position(shape).astype(jnp.float32) < counts[slots + slot : slots + slot + 1, :1]

    for stage in attend(inside, lambda slot, c, h: cache_ref[slot, c, h], q_scr, s_scr, p_scr, e_scr, m_scr, l_scr, kv_heads):
        for slot in range(slots):
            stage(slot)
    heads = gather_heads(e_scr, m_scr, l_scr, kv_heads, None)
    lane = lax.broadcasted_iota(jnp.int32, (8, LANES), 1)
    logs = jnp.zeros((8, LANES), jnp.float32)
    for j in range(len(heads) // 2):
        mixed = jnp.where(lane < HD, *[u / l for u, _, l in heads[2 * j : 2 * j + 2]])
        out_ref[:, j * LANES : (j + 1) * LANES] = mixed[:slots]
        for h in (2 * j, 2 * j + 1):
            _, m, l = heads[h]
            logs = jnp.where(lane == h, m + jnp.log(l), logs)
    out_ref[:, len(heads) // 2 * LANES :] = logs[:slots]


def project_kernel(meta_ref, home_ref, far_ref, w_ref, out_ref, *mix_ref):
    blocks, rows = home_ref.shape[1:3]
    slots = far_ref.shape[0]
    meta = meta_ref[...]
    picks = [meta[0, 1 + rows + k] for k in range(slots)]
    row_id = lax.broadcasted_iota(jnp.int32, (rows, LANES), 0)
    low = lax.broadcasted_iota(jnp.int32, (slots, LANES), 1) < HD
    logs = far_ref[:, blocks * LANES :]
    mixes = []
    for j in range(blocks):
        block_o = far_ref[:, j * LANES : (j + 1) * LANES]
        block_m = jnp.where(low, logs[:, 2 * j : 2 * j + 1], logs[:, 2 * j + 1 : 2 * j + 2])
        far_o = jnp.zeros((rows, LANES), jnp.float32)
        far_m = jnp.full((rows, LANES), LOW, jnp.float32)
        for k in range(slots):
            at = row_id == picks[k]
            far_o = jnp.where(at, block_o[k : k + 1], far_o)
            far_m = jnp.where(at, block_m[k : k + 1], far_m)
        u, m, l = home_ref[0, j], home_ref[1, j], home_ref[2, j]
        top = jnp.maximum(m, far_m)
        near, far = jnp.exp(m - top), jnp.exp(far_m - top)
        mixes.append((u * near + far_o * far) / (l * near + far))
    mix = jnp.concatenate(mixes, axis=1).astype(jnp.bfloat16)
    for ref in mix_ref:
        ref[...] = mix
    project(mix, w_ref, out_ref, 1 - lax.axis_index("tp") if mix_ref else 0)


def project(mix, w_ref, out_ref, part):
    width = out_ref.shape[1]
    tile = min(512, width)

    def columns(n, _):
        source = pl.ds(pl.multiple_of(part * width + n * tile, tile), tile)
        target = pl.ds(pl.multiple_of(n * tile, tile), tile)
        out_ref[:, target] = jnp.dot(mix, w_ref[:, source], preferred_element_type=jnp.float32)
        return 0

    lax.fori_loop(0, width // tile, columns, 0)


def own_kernel(mix_ref, w_ref, out_ref):
    project(mix_ref[...], w_ref, out_ref, lax.axis_index("tp"))


def scratch(slots, kv_heads, context):
    small = pltpu.VMEM((kv_heads * 64, LANES), jnp.float32)
    items = slots * max(kv_heads // 2, 1)
    return [
        small,
        pltpu.VMEM((items * 16, context), jnp.float32),
        pltpu.VMEM((items * 16, context), jnp.bfloat16),
        small,
        small,
        small,
    ]


def pack(lengths, split_at, helper_req, queries, home_cache, groups):
    rows, width = queries.shape
    _, _, kv_heads, context, lanes = home_cache.shape
    home_cache = home_cache.reshape(-1, context, lanes)
    small = jax.ShapeDtypeStruct((kv_heads * 64, LANES), jnp.float32)
    return pl.pallas_call(
        functools.partial(pack_kernel, groups=groups),
        out_shape=(
            jax.ShapeDtypeStruct((rows, width), jnp.bfloat16),
            jax.ShapeDtypeStruct((rows, LANES), jnp.int32),
            small,
            small,
            small,
        ),
        in_specs=[ANY] * 5,
        out_specs=(VMEM,) * 5,
        scratch_shapes=[
            pltpu.SMEM(lengths.shape, jnp.int32),
            pltpu.SMEM(split_at.shape, jnp.int32),
            pltpu.SMEM(helper_req.shape, jnp.int32),
            pltpu.VMEM(queries.shape, jnp.bfloat16),
            pltpu.SemaphoreType.DMA((4,)),
            pltpu.VMEM(home_cache.shape, jnp.bfloat16),
            pltpu.SemaphoreType.DMA((2 * rows,)),
        ]
        + scratch(rows, kv_heads, context)[:3],
        compiler_params=pltpu.CompilerParams(vmem_limit_bytes=60 * MIB),
        name="pack",
    )(lengths, split_at, helper_req, queries, home_cache)


def attention(packed, meta, early, queries, new_kv, home_cache, help_cache, out_weight, exchange, cores):
    rows, _, kv_heads, context, lanes = home_cache.shape
    slots = help_cache.shape[0]
    blocks = kv_heads * GROUP // 2
    home_cache = home_cache.reshape(-1, context, lanes)

    far_queries = exchange(packed)
    small = jax.ShapeDtypeStruct((kv_heads * 64, LANES), jnp.float32)
    sums = pl.pallas_call(
        home_kernel,
        out_shape=(small, small, small),
        in_specs=[VMEM] * 5 + [ANY],
        out_specs=(VMEM, VMEM, VMEM),
        scratch_shapes=[
            pltpu.SMEM((rows,), jnp.int32),
            pltpu.VMEM(home_cache.shape, jnp.bfloat16),
            pltpu.SemaphoreType.DMA((2 * rows,)),
        ]
        + scratch(rows, kv_heads, context)[:3],
        compiler_params=pltpu.CompilerParams(vmem_limit_bytes=32 * MIB),
        cost_estimate=pl.CostEstimate(
            flops=64 * home_cache.size, bytes_accessed=2 * home_cache.size, transcendentals=0
        ),
        name="home",
    )(meta, queries, *early, home_cache)
    partials = pl.pallas_call(
        help_kernel,
        out_shape=jax.ShapeDtypeStruct((slots, (blocks + 1) * LANES), jnp.float32),
        in_specs=[VMEM, ANY, VMEM],
        out_specs=VMEM,
        scratch_shapes=scratch(slots, kv_heads, context),
        compiler_params=pltpu.CompilerParams(vmem_limit_bytes=16 * MIB),
        name="help",
    )(far_queries, sums[0], help_cache)
    far = exchange(partials)
    home = pl.pallas_call(
        finish_kernel,
        out_shape=jax.ShapeDtypeStruct((3, blocks, rows, LANES), jnp.float32),
        in_specs=[VMEM] * 5 + [ANY],
        out_specs=VMEM,
        scratch_shapes=[pltpu.VMEM(small.shape, jnp.float32)],
        compiler_params=pltpu.CompilerParams(vmem_limit_bytes=16 * MIB),
        cost_estimate=pl.CostEstimate(flops=MIB, bytes_accessed=MIB, transcendentals=0),
        name="finish",
    )(queries, new_kv, *sums, partials)

    pair = cores == 2
    width = out_weight.shape[1] // (cores if pair else 1)
    partial = jax.ShapeDtypeStruct((rows, width), jnp.float32)
    mix = jax.ShapeDtypeStruct((rows, blocks * LANES), jnp.bfloat16)
    projected = pl.pallas_call(
        project_kernel,
        out_shape=(partial, mix) if pair else (partial,),
        in_specs=[VMEM] * 4,
        out_specs=(VMEM, VMEM) if pair else (VMEM,),
        compiler_params=pltpu.CompilerParams(vmem_limit_bytes=16 * MIB),
        name="project",
    )(meta, home, far, out_weight)
    if not pair:
        return projected[0]
    other = lax.ppermute(projected[0], "tp", [(0, 1), (1, 0)])
    own = pl.pallas_call(
        own_kernel,
        out_shape=partial,
        in_specs=[VMEM, VMEM],
        out_specs=VMEM,
        compiler_params=pltpu.CompilerParams(vmem_limit_bytes=16 * MIB),
        cost_estimate=pl.CostEstimate(
            flops=2 * rows * out_weight.size, bytes_accessed=out_weight.size, transcendentals=0
        ),
        name="own",
    )(projected[1], out_weight)
    return (own + other).astype(jnp.bfloat16)


def per_device(queries, new_kv, home_cache, help_cache, lengths, split_at, helper_req, out_weight):
    groups, cores = lax.axis_size("grp"), lax.axis_size("tp")
    partner = helper_req[0].astype(jnp.uint32) // queries.shape[0]
    distance = jnp.bitwise_xor(lax.axis_index("grp").astype(jnp.uint32), partner).astype(jnp.int32)
    packed, meta, *early = pack(lengths, split_at, helper_req, queries, home_cache, groups)
    arrays = (packed, meta, early, queries, new_kv, home_cache, help_cache, out_weight)
    if groups > MAX_BRANCHES:
        out = attention(*arrays, lambda x: lax.all_gather(x, "grp")[partner], cores)
    else:

        def at_distance(k):
            pairs = [(g, g ^ k) for g in range(groups)]
            return lambda *xs: attention(*xs, lambda x: lax.ppermute(x, "grp", pairs), cores)

        branches = [at_distance(k) for k in reversed(range(1, groups))]
        out = lax.switch(groups - 1 - distance, branches, *arrays)
    if cores == 2:
        return out
    return lax.psum_scatter(out, "tp", scatter_dimension=1, tiled=True).astype(jnp.bfloat16)


def solution(mesh):
    return jax.shard_map(
        per_device,
        mesh=mesh,
        in_specs=(
            P("grp", "tp"),
            P("grp", None, "tp"),
            P("grp", None, "tp", None, None),
            P("grp", None, "tp", None, None),
            P("grp"),
            P("grp"),
            P("grp"),
            P("tp", None),
        ),
        out_specs=P("grp", "tp"),
        check_vma=False,
    )
```

```python
import functools

import jax
import jax.numpy as jnp
from jax import lax
from jax.experimental import pallas as pl
from jax.experimental.pallas import tpu as pltpu
from jax.sharding import PartitionSpec as P

GROUP = 4
HD = 64
LANES = 2 * HD
CTX = 1024
LOW = -1e30
AT_ONCE = 4
STEP = 64
MIB = 1 << 20
MAX_BRANCHES = 32

VMEM = pl.BlockSpec(memory_space=pltpu.VMEM)
SMEM = pl.BlockSpec(memory_space=pltpu.SMEM)
ANY = pl.BlockSpec(memory_space=pl.ANY)


def long_rows(lengths, rows, slots):
    found = jnp.int32(0)
    picks = [jnp.int32(0)] * slots
    for r in range(rows):
        is_long = lengths[r] > CTX
        for k in range(slots):
            picks[k] = jnp.where(jnp.logical_and(is_long, found == k), jnp.int32(r), picks[k])
        found = found + is_long.astype(jnp.int32)
    return picks


def halves(x):
    low = lax.broadcasted_iota(jnp.int32, x.shape, x.ndim - 1) < HD
    swapped = pltpu.roll(x, HD, x.ndim - 1)
    return (
        (jnp.where(low, x, 0.0), jnp.where(low, 0.0, swapped)),
        (jnp.where(low, swapped, 0.0), jnp.where(low, 0.0, x)),
    )


def place_queries(x, q_scr, kv_heads):
    for j in range(kv_heads * GROUP // 2):
        block = halves(x[:, j * LANES : (j + 1) * LANES] * (HD**-0.5))
        for b in range(2):
            kv, i = divmod(2 * j + b, GROUP)
            for parity in range(2):
                q_scr[pl.ds((kv * 8 + parity * 4 + i) * 8, 8), :] = block[b][parity]


def attend(inside, block, q_scr, s_scr, p_scr, e_scr, m_scr, l_scr, kv_heads):
    pack = 2 if kv_heads % 2 == 0 else 1
    rows = 8 * pack
    items = kv_heads // pack

    def place(slot, h):
        return pl.ds(h * 64 + slot, 8, stride=8)

    def item_rows(slot, item):
        return pl.ds(pl.multiple_of((slot * items + item) * 16, 16), rows)

    def each(one):
        def stage(slot):
            for item in range(items):
                one(slot, item, range(item * pack, (item + 1) * pack))

        return stage

    def score(slot, item, heads):
        blocks = []
        for h in heads:
            part = q_scr[place(slot, h), :]
            zero = jnp.zeros_like(part)
            blocks.append(jnp.concatenate([part if o == h else zero for o in heads], axis=1))
        q = jnp.concatenate(blocks, axis=0).astype(jnp.bfloat16)
        keys = jnp.concatenate([block(slot, 0, h) for h in heads], axis=1)
        s = lax.dot_general(q, keys, (((1,), (1,)), ((), ())), preferred_element_type=jnp.float32)
        s_scr[item_rows(slot, item), :] = jnp.where(inside(slot, s.shape), s, LOW)

    def weigh(slot, item, heads):
        s = s_scr[item_rows(slot, item), :]
        m = jnp.max(s, axis=1, keepdims=True)
        p = jnp.exp(s - m).astype(jnp.bfloat16)
        p_scr[item_rows(slot, item), :] = p
        l = jnp.sum(p.astype(jnp.float32), axis=1, keepdims=True)
        for n, h in enumerate(heads):
            m_scr[place(slot, h), :] = jnp.broadcast_to(m[n * 8 : n * 8 + 8], (8, LANES))
            l_scr[place(slot, h), :] = jnp.broadcast_to(l[n * 8 : n * 8 + 8], (8, LANES))

    def mix(slot, item, heads):
        values = jnp.concatenate([block(slot, 1, h) for h in heads], axis=1)
        u = jnp.dot(p_scr[item_rows(slot, item), :], values, preferred_element_type=jnp.float32)
        for n, h in enumerate(heads):
            e_scr[place(slot, h), :] = u[n * 8 : n * 8 + 8, n * LANES : (n + 1) * LANES]

    return each(score), each(weigh), each(mix)


def position(shape):
    parity = (lax.broadcasted_iota(jnp.int32, shape, 0) // 4) % 2
    return 2 * lax.broadcasted_iota(jnp.int32, shape, 1) + parity


def heads_of(kv, e_scr, m_scr, l_scr, fresh):
    low = lax.broadcasted_iota(jnp.int32, (8, LANES), 1) < HD
    heads = []
    for i in range(GROUP):
        even = pl.ds(kv * 64 + i * 8, 8)
        odd = pl.ds(kv * 64 + (4 + i) * 8, 8)
        if not isinstance(kv, int):
            even, odd = [pl.ds(pl.multiple_of(at.start, 8), 8) for at in (even, odd)]
        m_even, m_odd = m_scr[even, :], m_scr[odd, :]
        m = jnp.maximum(m_even, m_odd)
        if fresh is not None:
            q_scr, new_key, new_value = fresh
            score = jnp.sum(q_scr[even, :] * new_key, axis=1, keepdims=True)
            m = jnp.maximum(m, score)
        by_even, by_odd = jnp.exp(m_even - m), jnp.exp(m_odd - m)
        l = l_scr[even, :] * by_even + l_scr[odd, :] * by_odd
        u = jnp.where(low, e_scr[even, :] * by_even, e_scr[odd, :] * by_odd)
        u = u + pltpu.roll(u, HD, 1)
        if fresh is not None:
            by_new = jnp.exp(score - m)
            l = l + by_new
            u = u + by_new * new_value
        heads.append((u, m, l))
    return heads


def attend_home(first, last, home_ref, cache, sems, count_ref, scratches, kv_heads):
    def slots_of(n):
        return [AT_ONCE * n + i for i in range(AT_ONCE)]

    def loop(body):
        def step(n, _):
            for slot in slots_of(n):
                body(slot)
            return 0

        lax.fori_loop(first, last, step, 0)

    def steps(slot):
        return (count_ref[slot] + (2 * STEP - 1)) >> STEP.bit_length()

    def copy(slot, c):
        at = pl.ds((2 * slot + c) * kv_heads, kv_heads)
        filled = pl.ds(0, pl.multiple_of(steps(slot) * STEP, STEP))
        return pltpu.make_async_copy(home_ref.at[at, filled], cache.at[at, filled], sems.at[2 * slot + c])

    def clear_rest(slot, _):
        def clear(n, _):
            at = pl.ds(pl.multiple_of(n * STEP, STEP), STEP)
            for h in range(kv_heads):
                cache[(2 * slot + 1) * kv_heads + h, at, :] = jnp.zeros((STEP, LANES), jnp.bfloat16)
            return 0

        return lax.fori_loop(steps(slot), cache.shape[1] // STEP, clear, 0)

    def inside(slot, shape):
        return position(shape) < count_ref[slot]

    score, weigh, mix = attend(
        inside, lambda slot, c, h: cache[(2 * slot + c) * kv_heads + h], *scratches, kv_heads
    )

    def begin(c):
        def one(slot, _):
            copy(slot, c).start()
            return 0

        lax.fori_loop(AT_ONCE * first, AT_ONCE * last, one, 0)

    def start():
        begin(0)
        begin(1)
        lax.fori_loop(AT_ONCE * first, AT_ONCE * last, clear_rest, 0)

    def step(c, stage):
        def body(n, _):
            for slot in slots_of(n):
                copy(slot, c).wait()
            for slot in slots_of(n):
                stage(slot)
            return 0

        lax.fori_loop(first, last, body, 0)

    def run():
        step(0, score)
        loop(weigh)
        step(1, mix)

    return start, run


def hops(group):
    return (group >> 2) + ((group >> 1) & 1) + (group & 1)


def pack_kernel(
    lengths_in, split_in, helper_in, q_in, home_ref,
    out_ref, meta_ref, e_ref, m_ref, l_ref,
    lengths_ref, split_ref, helper_ref, q_ref, in_sems, cache, sems, q_scr, s_scr, p_scr, *, groups,
):
    arrays = ((helper_in, helper_ref), (split_in, split_ref), (lengths_in, lengths_ref), (q_in, q_ref))
    copies = [pltpu.make_async_copy(*pair, in_sems.at[n]) for n, pair in enumerate(arrays)]
    for copy in copies:
        copy.start()
    for copy in copies:
        copy.wait()
    rows = q_ref.shape[0]
    kv_heads = home_ref.shape[0] // (2 * rows)
    slots = rows // 2
    me = lax.axis_index("grp")
    partner = lax.div(helper_ref[0], rows) if rows & (rows - 1) else helper_ref[0] >> (rows.bit_length() - 1)
    done = jnp.int32(0)
    if groups == 16:
        done = (hops(partner) - hops(me) > 2).astype(jnp.int32)
    scratches = (q_scr, s_scr, p_scr, e_ref, m_ref, l_ref)
    start, run = attend_home(0, done, home_ref, cache, sems, split_ref, scratches, kv_heads)

    @pl.when(done > 0)
    def _():
        start()

    picks = long_rows(lengths_ref, rows, slots)
    q = q_ref[...].astype(jnp.float32)
    row_id = lax.broadcasted_iota(jnp.int32, (rows, 1), 0)
    left = lax.broadcasted_iota(jnp.int32, q.shape, 1) < LANES
    meta_lane = lax.broadcasted_iota(jnp.int32, meta_ref.shape, 1)
    packed = jnp.zeros_like(q)
    meta = jnp.zeros(meta_ref.shape, jnp.int32)
    for k in range(slots):
        row = jnp.sum(jnp.where(row_id == picks[k], q, 0.0), axis=0, keepdims=True)
        packed = jnp.where(row_id == k, row, packed)
        count = lengths_ref[picks[k]] - split_ref[picks[k]]
        parts = jnp.where(left, (count >> 5).astype(jnp.float32), (count & 31).astype(jnp.float32))
        packed = jnp.where(row_id == slots + k, parts, packed)
        meta = jnp.where(meta_lane == 1 + rows + k, picks[k], meta)
    for r in range(rows):
        meta = jnp.where(meta_lane == 1 + r, split_ref[r], meta)
    out_ref[...] = packed.astype(jnp.bfloat16)
    meta_ref[...] = jnp.where(meta_lane == 1 + rows + slots, done, meta)

    @pl.when(done > 0)
    def _():
        place_queries(q, q_scr, kv_heads)
        run()


def home_kernel(
    meta_ref, q_ref, e_ref, m_ref, l_ref, home_ref, e_out, m_out, l_out, count_ref, cache, sems, q_scr, s_scr, p_scr
):
    rows = q_ref.shape[0]
    kv_heads = home_ref.shape[0] // (2 * rows)
    meta = meta_ref[...]
    done = meta[0, 1 + rows + rows // 2]
    scratches = (q_scr, s_scr, p_scr, e_out, m_out, l_out)
    start, run = attend_home(done, rows // AT_ONCE, home_ref, cache, sems, count_ref, scratches, kv_heads)
    for r in range(rows):
        count_ref[r] = meta[0, 1 + r]
    start()
    place_queries(q_ref[...].astype(jnp.float32), q_scr, kv_heads)

    @pl.when(done > 0)
    def _():
        for out, ref in ((e_out, e_ref), (m_out, m_ref), (l_out, l_ref)):
            out[...] = ref[...]

    run()


def finish_kernel(q_ref, new_ref, e_ref, m_ref, l_ref, after_ref, out_ref, q_scr, new_scr):
    kv_heads = q_ref.shape[1] // (GROUP * HD)
    place_queries(q_ref[...].astype(jnp.float32), q_scr, kv_heads)
    low = lax.broadcasted_iota(jnp.int32, (8, LANES), 1) < HD
    new = new_ref[...].astype(jnp.float32)
    for c in range(2):
        for kv in range(kv_heads):
            at = kv * HD // LANES * LANES
            width = min(LANES, kv_heads * HD)
            x = new[:, c, at : at + width]
            if width < LANES:
                x = jnp.concatenate([x, x], axis=1)
            swapped = pltpu.roll(x, HD, 1)
            both = jnp.where(low, x, swapped) if kv % 2 == 0 else jnp.where(low, swapped, x)
            new_scr[c, pl.ds(kv * 8, 8), :] = both

    def one(kv, _):
        at = pl.ds(pl.multiple_of(kv * 8, 8), 8)
        heads = heads_of(kv, e_ref, m_ref, l_ref, (q_scr, new_scr[0, at, :], new_scr[1, at, :]))
        for b in range(GROUP // 2):
            for n in range(3):
                out_ref[n, kv * (GROUP // 2) + b] = jnp.where(low, heads[2 * b][n], heads[2 * b + 1][n])
        return 0

    lax.fori_loop(0, kv_heads, one, 0)


def help_kernel(far_ref, after_ref, cache_ref, out_ref, q_scr, s_scr, p_scr, e_scr, m_scr, l_scr):
    slots = out_ref.shape[0]
    kv_heads = cache_ref.shape[2]
    far = far_ref[...].astype(jnp.float32)
    counts = far[:, :LANES] * 32.0 + far[:, LANES : 2 * LANES]
    place_queries(far, q_scr, kv_heads)

    def inside(slot, shape):
        return position(shape).astype(jnp.float32) < counts[slots + slot : slots + slot + 1, :1]

    for stage in attend(inside, lambda slot, c, h: cache_ref[slot, c, h], q_scr, s_scr, p_scr, e_scr, m_scr, l_scr, kv_heads):
        for slot in range(slots):
            stage(slot)
    heads = [head for kv in range(kv_heads) for head in heads_of(kv, e_scr, m_scr, l_scr, None)]
    lane = lax.broadcasted_iota(jnp.int32, (8, LANES), 1)
    logs = jnp.zeros((8, LANES), jnp.float32)
    for j in range(len(heads) // 2):
        mixed = jnp.where(lane < HD, *[u / l for u, _, l in heads[2 * j : 2 * j + 2]])
        out_ref[:, j * LANES : (j + 1) * LANES] = mixed[:slots]
        for h in (2 * j, 2 * j + 1):
            _, m, l = heads[h]
            logs = jnp.where(lane == h, m + jnp.log(l), logs)
    out_ref[:, len(heads) // 2 * LANES :] = logs[:slots]


def project_kernel(meta_ref, home_ref, far_ref, w_ref, out_ref, *mix_ref):
    blocks, rows = home_ref.shape[1:3]
    slots = far_ref.shape[0]
    meta = meta_ref[...]
    picks = [meta[0, 1 + rows + k] for k in range(slots)]
    row_id = lax.broadcasted_iota(jnp.int32, (rows, LANES), 0)
    low = lax.broadcasted_iota(jnp.int32, (slots, LANES), 1) < HD
    logs = far_ref[:, blocks * LANES :]
    mixes = []
    for j in range(blocks):
        block_o = far_ref[:, j * LANES : (j + 1) * LANES]
        block_m = jnp.where(low, logs[:, 2 * j : 2 * j + 1], logs[:, 2 * j + 1 : 2 * j + 2])
        far_o = jnp.zeros((rows, LANES), jnp.float32)
        far_m = jnp.full((rows, LANES), LOW, jnp.float32)
        for k in range(slots):
            at = row_id == picks[k]
            far_o = jnp.where(at, block_o[k : k + 1], far_o)
            far_m = jnp.where(at, block_m[k : k + 1], far_m)
        u, m, l = home_ref[0, j], home_ref[1, j], home_ref[2, j]
        top = jnp.maximum(m, far_m)
        near, far = jnp.exp(m - top), jnp.exp(far_m - top)
        mixes.append((u * near + far_o * far) / (l * near + far))
    mix = jnp.concatenate(mixes, axis=1).astype(jnp.bfloat16)
    for ref in mix_ref:
        ref[...] = mix
    project(mix, w_ref, out_ref, 1 - lax.axis_index("tp") if mix_ref else 0)


def project(mix, w_ref, out_ref, part):
    width = out_ref.shape[1]
    tile = min(512, width)

    def columns(n, _):
        source = pl.ds(pl.multiple_of(part * width + n * tile, tile), tile)
        target = pl.ds(pl.multiple_of(n * tile, tile), tile)
        out_ref[:, target] = jnp.dot(mix, w_ref[:, source], preferred_element_type=jnp.float32)
        return 0

    lax.fori_loop(0, width // tile, columns, 0)


def own_kernel(mix_ref, w_ref, out_ref):
    project(mix_ref[...], w_ref, out_ref, lax.axis_index("tp"))


def scratch(slots, kv_heads, context):
    small = pltpu.VMEM((kv_heads * 64, LANES), jnp.float32)
    items = slots * max(kv_heads // 2, 1)
    return [
        small,
        pltpu.VMEM((items * 16, context), jnp.float32),
        pltpu.VMEM((items * 16, context), jnp.bfloat16),
        small,
        small,
        small,
    ]


def pack(lengths, split_at, helper_req, queries, home_cache, groups):
    rows, width = queries.shape
    _, _, kv_heads, context, lanes = home_cache.shape
    home_cache = home_cache.reshape(-1, context, lanes)
    small = jax.ShapeDtypeStruct((kv_heads * 64, LANES), jnp.float32)
    return pl.pallas_call(
        functools.partial(pack_kernel, groups=groups),
        out_shape=(
            jax.ShapeDtypeStruct((rows, width), jnp.bfloat16),
            jax.ShapeDtypeStruct((rows, LANES), jnp.int32),
            small,
            small,
            small,
        ),
        in_specs=[ANY] * 5,
        out_specs=(VMEM,) * 5,
        scratch_shapes=[
            pltpu.SMEM(lengths.shape, jnp.int32),
            pltpu.SMEM(split_at.shape, jnp.int32),
            pltpu.SMEM(helper_req.shape, jnp.int32),
            pltpu.VMEM(queries.shape, jnp.bfloat16),
            pltpu.SemaphoreType.DMA((4,)),
            pltpu.VMEM(home_cache.shape, jnp.bfloat16),
            pltpu.SemaphoreType.DMA((2 * rows,)),
        ]
        + scratch(rows, kv_heads, context)[:3],
        compiler_params=pltpu.CompilerParams(vmem_limit_bytes=60 * MIB),
        name="pack",
    )(lengths, split_at, helper_req, queries, home_cache)


def attention(packed, meta, early, queries, new_kv, home_cache, help_cache, out_weight, exchange, cores):
    rows, _, kv_heads, context, lanes = home_cache.shape
    slots = help_cache.shape[0]
    blocks = kv_heads * GROUP // 2
    home_cache = home_cache.reshape(-1, context, lanes)

    far_queries = exchange(packed)
    small = jax.ShapeDtypeStruct((kv_heads * 64, LANES), jnp.float32)
    sums = pl.pallas_call(
        home_kernel,
        out_shape=(small, small, small),
        in_specs=[VMEM] * 5 + [ANY],
        out_specs=(VMEM, VMEM, VMEM),
        scratch_shapes=[
            pltpu.SMEM((rows,), jnp.int32),
            pltpu.VMEM(home_cache.shape, jnp.bfloat16),
            pltpu.SemaphoreType.DMA((2 * rows,)),
        ]
        + scratch(rows, kv_heads, context)[:3],
        compiler_params=pltpu.CompilerParams(vmem_limit_bytes=32 * MIB),
        cost_estimate=pl.CostEstimate(
            flops=64 * home_cache.size, bytes_accessed=2 * home_cache.size, transcendentals=0
        ),
        name="home",
    )(meta, queries, *early, home_cache)
    partials = pl.pallas_call(
        help_kernel,
        out_shape=jax.ShapeDtypeStruct((slots, (blocks + 1) * LANES), jnp.float32),
        in_specs=[VMEM, ANY, VMEM],
        out_specs=VMEM,
        scratch_shapes=scratch(slots, kv_heads, context),
        compiler_params=pltpu.CompilerParams(vmem_limit_bytes=16 * MIB),
        name="help",
    )(far_queries, sums[0], help_cache)
    far = exchange(partials)
    home = pl.pallas_call(
        finish_kernel,
        out_shape=jax.ShapeDtypeStruct((3, blocks, rows, LANES), jnp.float32),
        in_specs=[VMEM] * 5 + [ANY],
        out_specs=VMEM,
        scratch_shapes=[
            pltpu.VMEM(small.shape, jnp.float32),
            pltpu.VMEM((2, kv_heads * 8, LANES), jnp.float32),
        ],
        compiler_params=pltpu.CompilerParams(vmem_limit_bytes=16 * MIB),
        cost_estimate=pl.CostEstimate(flops=MIB, bytes_accessed=MIB, transcendentals=0),
        name="finish",
    )(queries, new_kv, *sums, partials)

    pair = cores == 2
    width = out_weight.shape[1] // (cores if pair else 1)
    partial = jax.ShapeDtypeStruct((rows, width), jnp.float32)
    mix = jax.ShapeDtypeStruct((rows, blocks * LANES), jnp.bfloat16)
    projected = pl.pallas_call(
        project_kernel,
        out_shape=(partial, mix) if pair else (partial,),
        in_specs=[VMEM] * 4,
        out_specs=(VMEM, VMEM) if pair else (VMEM,),
        compiler_params=pltpu.CompilerParams(vmem_limit_bytes=16 * MIB),
        name="project",
    )(meta, home, far, out_weight)
    if not pair:
        return projected[0]
    other = lax.ppermute(projected[0], "tp", [(0, 1), (1, 0)])
    own = pl.pallas_call(
        own_kernel,
        out_shape=partial,
        in_specs=[VMEM, VMEM],
        out_specs=VMEM,
        compiler_params=pltpu.CompilerParams(vmem_limit_bytes=16 * MIB),
        cost_estimate=pl.CostEstimate(
            flops=2 * rows * out_weight.size, bytes_accessed=out_weight.size, transcendentals=0
        ),
        name="own",
    )(projected[1], out_weight)
    return (own + other).astype(jnp.bfloat16)


def per_device(queries, new_kv, home_cache, help_cache, lengths, split_at, helper_req, out_weight):
    groups, cores = lax.axis_size("grp"), lax.axis_size("tp")
    partner = helper_req[0].astype(jnp.uint32) // queries.shape[0]
    distance = jnp.bitwise_xor(lax.axis_index("grp").astype(jnp.uint32), partner).astype(jnp.int32)
    packed, meta, *early = pack(lengths, split_at, helper_req, queries, home_cache, groups)
    arrays = (packed, meta, early, queries, new_kv, home_cache, help_cache, out_weight)
    if groups > MAX_BRANCHES:
        out = attention(*arrays, lambda x: lax.all_gather(x, "grp")[partner], cores)
    else:

        def at_distance(k):
            pairs = [(g, g ^ k) for g in range(groups)]
            return lambda *xs: attention(*xs, lambda x: lax.ppermute(x, "grp", pairs), cores)

        branches = [at_distance(k) for k in reversed(range(1, groups))]
        out = lax.switch(groups - 1 - distance, branches, *arrays)
    if cores == 2:
        return out
    return lax.psum_scatter(out, "tp", scatter_dimension=1, tiled=True).astype(jnp.bfloat16)


def solution(mesh):
    return jax.shard_map(
        per_device,
        mesh=mesh,
        in_specs=(
            P("grp", "tp"),
            P("grp", None, "tp"),
            P("grp", None, "tp", None, None),
            P("grp", None, "tp", None, None),
            P("grp"),
            P("grp"),
            P("grp"),
            P("tp", None),
        ),
        out_specs=P("grp", "tp"),
        check_vma=False,
    )
```

```python
import functools

import jax
import jax.numpy as jnp
from jax import lax
from jax.experimental import pallas as pl
from jax.experimental.pallas import tpu as pltpu
from jax.sharding import PartitionSpec as P

GROUP = 4
HD = 64
LANES = 2 * HD
CTX = 1024
LOW = -1e30
AT_ONCE = 4
STEP = 128
MIB = 1 << 20
MAX_BRANCHES = 32

VMEM = pl.BlockSpec(memory_space=pltpu.VMEM)
SMEM = pl.BlockSpec(memory_space=pltpu.SMEM)
ANY = pl.BlockSpec(memory_space=pl.ANY)


def long_rows(lengths, rows, slots):
    found = jnp.int32(0)
    picks = [jnp.int32(0)] * slots
    for r in range(rows):
        is_long = lengths[r] > CTX
        for k in range(slots):
            picks[k] = jnp.where(jnp.logical_and(is_long, found == k), jnp.int32(r), picks[k])
        found = found + is_long.astype(jnp.int32)
    return picks


def halves(x):
    low = lax.broadcasted_iota(jnp.int32, x.shape, x.ndim - 1) < HD
    swapped = pltpu.roll(x, HD, x.ndim - 1)
    return (
        (jnp.where(low, x, 0.0), jnp.where(low, 0.0, swapped)),
        (jnp.where(low, swapped, 0.0), jnp.where(low, 0.0, x)),
    )


def place_queries(x, q_scr, kv_heads):
    for j in range(kv_heads * GROUP // 2):
        block = halves(x[:, j * LANES : (j + 1) * LANES] * (HD**-0.5))
        for b in range(2):
            kv, i = divmod(2 * j + b, GROUP)
            for parity in range(2):
                q_scr[pl.ds((kv * 8 + parity * 4 + i) * 8, 8), :] = block[b][parity]


def attend(inside, block, q_scr, s_scr, p_scr, e_scr, m_scr, l_scr, kv_heads):
    pack = 2 if kv_heads % 2 == 0 else 1
    rows = 8 * pack
    items = kv_heads // pack

    def place(slot, h):
        return pl.ds(h * 64 + slot, 8, stride=8)

    def item_rows(slot, item):
        return pl.ds(pl.multiple_of((slot * items + item) * 16, 16), rows)

    def each(one):
        def stage(slot):
            for item in range(items):
                one(slot, item, range(item * pack, (item + 1) * pack))

        return stage

    def score(slot, item, heads):
        blocks = []
        for h in heads:
            part = q_scr[place(slot, h), :]
            zero = jnp.zeros_like(part)
            blocks.append(jnp.concatenate([part if o == h else zero for o in heads], axis=1))
        q = jnp.concatenate(blocks, axis=0).astype(jnp.bfloat16)
        keys = jnp.concatenate([block(slot, 0, h) for h in heads], axis=1)
        s = lax.dot_general(q, keys, (((1,), (1,)), ((), ())), preferred_element_type=jnp.float32)
        s_scr[item_rows(slot, item), :] = jnp.where(inside(slot, s.shape), s, LOW)

    def weigh(slot, item, heads):
        s = s_scr[item_rows(slot, item), :]
        m = jnp.max(s, axis=1, keepdims=True)
        p = jnp.exp(s - m).astype(jnp.bfloat16)
        p_scr[item_rows(slot, item), :] = p
        l = jnp.sum(p.astype(jnp.float32), axis=1, keepdims=True)
        for n, h in enumerate(heads):
            m_scr[place(slot, h), :] = jnp.broadcast_to(m[n * 8 : n * 8 + 8], (8, LANES))
            l_scr[place(slot, h), :] = jnp.broadcast_to(l[n * 8 : n * 8 + 8], (8, LANES))

    def mix(slot, item, heads):
        values = jnp.concatenate([block(slot, 1, h) for h in heads], axis=1)
        u = jnp.dot(p_scr[item_rows(slot, item), :], values, preferred_element_type=jnp.float32)
        for n, h in enumerate(heads):
            e_scr[place(slot, h), :] = u[n * 8 : n * 8 + 8, n * LANES : (n + 1) * LANES]

    return each(score), each(weigh), each(mix)


def position(shape):
    parity = (lax.broadcasted_iota(jnp.int32, shape, 0) // 4) % 2
    return 2 * lax.broadcasted_iota(jnp.int32, shape, 1) + parity


def gather_heads(e_scr, m_scr, l_scr, kv_heads, fresh):
    low = lax.broadcasted_iota(jnp.int32, (8, LANES), 1) < HD
    heads = []
    for kv in range(kv_heads):
        for i in range(GROUP):
            even = pl.ds((kv * 8 + i) * 8, 8)
            odd = pl.ds((kv * 8 + 4 + i) * 8, 8)
            m_even, m_odd = m_scr[even, :], m_scr[odd, :]
            m = jnp.maximum(m_even, m_odd)
            if fresh is not None:
                q_scr, new_keys, new_values = fresh
                score = jnp.sum(q_scr[even, :] * new_keys[kv], axis=1, keepdims=True)
                m = jnp.maximum(m, score)
            by_even, by_odd = jnp.exp(m_even - m), jnp.exp(m_odd - m)
            l = l_scr[even, :] * by_even + l_scr[odd, :] * by_odd
            u = jnp.where(low, e_scr[even, :] * by_even, e_scr[odd, :] * by_odd)
            u = u + pltpu.roll(u, HD, 1)
            if fresh is not None:
                by_new = jnp.exp(score - m)
                l = l + by_new
                u = u + by_new * new_values[kv]
            heads.append((u, m, l))
    return heads


def attend_home(first, last, home_ref, cache, sems, count_ref, scratches, kv_heads):
    def slots_of(n):
        return [AT_ONCE * n + i for i in range(AT_ONCE)]

    def loop(body):
        def step(n, _):
            for slot in slots_of(n):
                body(slot)
            return 0

        lax.fori_loop(first, last, step, 0)

    def steps(slot):
        return (count_ref[slot] + (2 * STEP - 1)) >> STEP.bit_length()

    def copy(slot, c):
        at = pl.ds((2 * slot + c) * kv_heads, kv_heads)
        filled = pl.ds(0, pl.multiple_of(steps(slot) * STEP, STEP))
        return pltpu.make_async_copy(home_ref.at[at, filled], cache.at[at, filled], sems.at[2 * slot + c])

    def clear_rest(slot, _):
        def clear(n, _):
            at = pl.ds(pl.multiple_of(n * STEP, STEP), STEP)
            for h in range(kv_heads):
                cache[(2 * slot + 1) * kv_heads + h, at, :] = jnp.zeros((STEP, LANES), jnp.bfloat16)
            return 0

        return lax.fori_loop(steps(slot), cache.shape[1] // STEP, clear, 0)

    def inside(slot, shape):
        return position(shape) < count_ref[slot]

    score, weigh, mix = attend(
        inside, lambda slot, c, h: cache[(2 * slot + c) * kv_heads + h], *scratches, kv_heads
    )

    def begin(c):
        def one(slot, _):
            copy(slot, c).start()
            return 0

        lax.fori_loop(AT_ONCE * first, AT_ONCE * last, one, 0)

    def start():
        begin(0)
        begin(1)
        lax.fori_loop(AT_ONCE * first, AT_ONCE * last, clear_rest, 0)

    def step(c, stage):
        def body(n, _):
            for slot in slots_of(n):
                copy(slot, c).wait()
            for slot in slots_of(n):
                stage(slot)
            return 0

        lax.fori_loop(first, last, body, 0)

    def run():
        step(0, score)
        loop(weigh)
        step(1, mix)

    return start, run


def hops(group):
    return (group >> 2) + ((group >> 1) & 1) + (group & 1)


def pack_kernel(
    lengths_in, split_in, helper_in, q_in, home_ref,
    out_ref, meta_ref, e_ref, m_ref, l_ref,
    lengths_ref, split_ref, helper_ref, q_ref, in_sems, cache, sems, q_scr, s_scr, p_scr, *, groups,
):
    arrays = ((helper_in, helper_ref), (split_in, split_ref), (lengths_in, lengths_ref), (q_in, q_ref))
    copies = [pltpu.make_async_copy(*pair, in_sems.at[n]) for n, pair in enumerate(arrays)]
    for copy in copies:
        copy.start()
    for copy in copies:
        copy.wait()
    rows = q_ref.shape[0]
    kv_heads = home_ref.shape[0] // (2 * rows)
    slots = rows // 2
    me = lax.axis_index("grp")
    partner = helper_ref[0] // rows
    done = jnp.int32(0)
    if groups == 16:
        done = (hops(partner) - hops(me) > 2).astype(jnp.int32)
    scratches = (q_scr, s_scr, p_scr, e_ref, m_ref, l_ref)
    start, run = attend_home(0, done, home_ref, cache, sems, split_ref, scratches, kv_heads)

    @pl.when(done > 0)
    def _():
        start()

    picks = long_rows(lengths_ref, rows, slots)
    q = q_ref[...].astype(jnp.float32)
    row_id = lax.broadcasted_iota(jnp.int32, (rows, 1), 0)
    left = lax.broadcasted_iota(jnp.int32, q.shape, 1) < LANES
    meta_lane = lax.broadcasted_iota(jnp.int32, meta_ref.shape, 1)
    packed = jnp.zeros_like(q)
    meta = jnp.zeros(meta_ref.shape, jnp.int32)
    for k in range(slots):
        row = jnp.sum(jnp.where(row_id == picks[k], q, 0.0), axis=0, keepdims=True)
        packed = jnp.where(row_id == k, row, packed)
        count = lengths_ref[picks[k]] - split_ref[picks[k]]
        parts = jnp.where(left, (count >> 5).astype(jnp.float32), (count & 31).astype(jnp.float32))
        packed = jnp.where(row_id == slots + k, parts, packed)
        meta = jnp.where(meta_lane == 1 + rows + k, picks[k], meta)
    for r in range(rows):
        meta = jnp.where(meta_lane == 1 + r, split_ref[r], meta)
    out_ref[...] = packed.astype(jnp.bfloat16)
    meta_ref[...] = jnp.where(meta_lane == 1 + rows + slots, done, meta)

    @pl.when(done > 0)
    def _():
        place_queries(q, q_scr, kv_heads)
        run()


def home_kernel(
    meta_ref, q_ref, e_ref, m_ref, l_ref, home_ref, e_out, m_out, l_out, count_ref, cache, sems, q_scr, s_scr, p_scr
):
    rows = q_ref.shape[0]
    kv_heads = home_ref.shape[0] // (2 * rows)
    meta = meta_ref[...]
    done = meta[0, 1 + rows + rows // 2]
    scratches = (q_scr, s_scr, p_scr, e_out, m_out, l_out)
    start, run = attend_home(done, rows // AT_ONCE, home_ref, cache, sems, count_ref, scratches, kv_heads)
    for r in range(rows):
        count_ref[r] = meta[0, 1 + r]
    start()
    place_queries(q_ref[...].astype(jnp.float32), q_scr, kv_heads)

    @pl.when(done > 0)
    def _():
        for out, ref in ((e_out, e_ref), (m_out, m_ref), (l_out, l_ref)):
            out[...] = ref[...]

    run()


def finish_kernel(q_ref, new_ref, e_ref, m_ref, l_ref, after_ref, out_ref, q_scr):
    kv_heads = q_ref.shape[1] // (GROUP * HD)
    place_queries(q_ref[...].astype(jnp.float32), q_scr, kv_heads)
    low = lax.broadcasted_iota(jnp.int32, (8, LANES), 1) < HD
    new = new_ref[...].astype(jnp.float32)
    fresh = []
    for c in range(2):
        per_kv = []
        for kv in range(kv_heads):
            at = kv * HD // LANES * LANES
            width = min(LANES, kv_heads * HD)
            x = new[:, c, at : at + width]
            if width < LANES:
                x = jnp.concatenate([x, x], axis=1)
            swapped = pltpu.roll(x, HD, 1)
            per_kv.append(jnp.where(low, x, swapped) if kv % 2 == 0 else jnp.where(low, swapped, x))
        fresh.append(per_kv)
    heads = gather_heads(e_ref, m_ref, l_ref, kv_heads, (q_scr, *fresh))
    for j in range(len(heads) // 2):
        for n in range(3):
            out_ref[n, j] = jnp.where(low, heads[2 * j][n], heads[2 * j + 1][n])


def help_kernel(far_ref, after_ref, cache_ref, out_ref, q_scr, s_scr, p_scr, e_scr, m_scr, l_scr):
    slots = out_ref.shape[0]
    kv_heads = cache_ref.shape[2]
    far = far_ref[...].astype(jnp.float32)
    counts = far[:, :LANES] * 32.0 + far[:, LANES : 2 * LANES]
    place_queries(far, q_scr, kv_heads)

    def inside(slot, shape):
        return position(shape).astype(jnp.float32) < counts[slots + slot : slots + slot + 1, :1]

    for stage in attend(inside, lambda slot, c, h: cache_ref[slot, c, h], q_scr, s_scr, p_scr, e_scr, m_scr, l_scr, kv_heads):
        for slot in range(slots):
            stage(slot)
    heads = gather_heads(e_scr, m_scr, l_scr, kv_heads, None)
    lane = lax.broadcasted_iota(jnp.int32, (8, LANES), 1)
    logs = jnp.zeros((8, LANES), jnp.float32)
    for j in range(len(heads) // 2):
        mixed = jnp.where(lane < HD, *[u / l for u, _, l in heads[2 * j : 2 * j + 2]])
        out_ref[:, j * LANES : (j + 1) * LANES] = mixed[:slots]
        for h in (2 * j, 2 * j + 1):
            _, m, l = heads[h]
            logs = jnp.where(lane == h, m + jnp.log(l), logs)
    out_ref[:, len(heads) // 2 * LANES :] = logs[:slots]


def project_kernel(meta_ref, home_ref, far_ref, w_ref, out_ref, *mix_ref):
    blocks, rows = home_ref.shape[1:3]
    slots = far_ref.shape[0]
    meta = meta_ref[...]
    picks = [meta[0, 1 + rows + k] for k in range(slots)]
    row_id = lax.broadcasted_iota(jnp.int32, (rows, LANES), 0)
    low = lax.broadcasted_iota(jnp.int32, (slots, LANES), 1) < HD
    logs = far_ref[:, blocks * LANES :]
    mixes = []
    for j in range(blocks):
        block_o = far_ref[:, j * LANES : (j + 1) * LANES]
        block_m = jnp.where(low, logs[:, 2 * j : 2 * j + 1], logs[:, 2 * j + 1 : 2 * j + 2])
        far_o = jnp.zeros((rows, LANES), jnp.float32)
        far_m = jnp.full((rows, LANES), LOW, jnp.float32)
        for k in range(slots):
            at = row_id == picks[k]
            far_o = jnp.where(at, block_o[k : k + 1], far_o)
            far_m = jnp.where(at, block_m[k : k + 1], far_m)
        u, m, l = home_ref[0, j], home_ref[1, j], home_ref[2, j]
        top = jnp.maximum(m, far_m)
        near, far = jnp.exp(m - top), jnp.exp(far_m - top)
        mixes.append((u * near + far_o * far) / (l * near + far))
    mix = jnp.concatenate(mixes, axis=1).astype(jnp.bfloat16)
    for ref in mix_ref:
        ref[...] = mix
    project(mix, w_ref, out_ref, 1 - lax.axis_index("tp") if mix_ref else 0)


def project(mix, w_ref, out_ref, part):
    width = out_ref.shape[1]
    tile = min(512, width)

    def columns(n, _):
        source = pl.ds(pl.multiple_of(part * width + n * tile, tile), tile)
        target = pl.ds(pl.multiple_of(n * tile, tile), tile)
        out_ref[:, target] = jnp.dot(mix, w_ref[:, source], preferred_element_type=jnp.float32)
        return 0

    lax.fori_loop(0, width // tile, columns, 0)


def own_kernel(mix_ref, w_ref, out_ref):
    project(mix_ref[...], w_ref, out_ref, lax.axis_index("tp"))


def scratch(slots, kv_heads, context):
    small = pltpu.VMEM((kv_heads * 64, LANES), jnp.float32)
    items = slots * max(kv_heads // 2, 1)
    return [
        small,
        pltpu.VMEM((items * 16, context), jnp.float32),
        pltpu.VMEM((items * 16, context), jnp.bfloat16),
        small,
        small,
        small,
    ]


def pack(lengths, split_at, helper_req, queries, home_cache, groups):
    rows, width = queries.shape
    _, _, kv_heads, context, lanes = home_cache.shape
    home_cache = home_cache.reshape(-1, context, lanes)
    small = jax.ShapeDtypeStruct((kv_heads * 64, LANES), jnp.float32)
    return pl.pallas_call(
        functools.partial(pack_kernel, groups=groups),
        out_shape=(
            jax.ShapeDtypeStruct((rows, width), jnp.bfloat16),
            jax.ShapeDtypeStruct((rows, LANES), jnp.int32),
            small,
            small,
            small,
        ),
        in_specs=[ANY] * 5,
        out_specs=(VMEM,) * 5,
        scratch_shapes=[
            pltpu.SMEM(lengths.shape, jnp.int32),
            pltpu.SMEM(split_at.shape, jnp.int32),
            pltpu.SMEM(helper_req.shape, jnp.int32),
            pltpu.VMEM(queries.shape, jnp.bfloat16),
            pltpu.SemaphoreType.DMA((4,)),
            pltpu.VMEM(home_cache.shape, jnp.bfloat16),
            pltpu.SemaphoreType.DMA((2 * rows,)),
        ]
        + scratch(rows, kv_heads, context)[:3],
        compiler_params=pltpu.CompilerParams(vmem_limit_bytes=60 * MIB),
        name="pack",
    )(lengths, split_at, helper_req, queries, home_cache)


def attention(packed, meta, early, queries, new_kv, home_cache, help_cache, out_weight, exchange, cores):
    rows, _, kv_heads, context, lanes = home_cache.shape
    slots = help_cache.shape[0]
    blocks = kv_heads * GROUP // 2
    home_cache = home_cache.reshape(-1, context, lanes)

    far_queries = exchange(packed)
    small = jax.ShapeDtypeStruct((kv_heads * 64, LANES), jnp.float32)
    sums = pl.pallas_call(
        home_kernel,
        out_shape=(small, small, small),
        in_specs=[VMEM] * 5 + [ANY],
        out_specs=(VMEM, VMEM, VMEM),
        scratch_shapes=[
            pltpu.SMEM((rows,), jnp.int32),
            pltpu.VMEM(home_cache.shape, jnp.bfloat16),
            pltpu.SemaphoreType.DMA((2 * rows,)),
        ]
        + scratch(rows, kv_heads, context)[:3],
        compiler_params=pltpu.CompilerParams(vmem_limit_bytes=32 * MIB),
        cost_estimate=pl.CostEstimate(
            flops=64 * home_cache.size, bytes_accessed=2 * home_cache.size, transcendentals=0
        ),
        name="home",
    )(meta, queries, *early, home_cache)
    partials = pl.pallas_call(
        help_kernel,
        out_shape=jax.ShapeDtypeStruct((slots, (blocks + 1) * LANES), jnp.float32),
        in_specs=[VMEM, ANY, VMEM],
        out_specs=VMEM,
        scratch_shapes=scratch(slots, kv_heads, context),
        compiler_params=pltpu.CompilerParams(vmem_limit_bytes=16 * MIB),
        name="help",
    )(far_queries, sums[0], help_cache)
    far = exchange(partials)
    home = pl.pallas_call(
        finish_kernel,
        out_shape=jax.ShapeDtypeStruct((3, blocks, rows, LANES), jnp.float32),
        in_specs=[VMEM] * 5 + [ANY],
        out_specs=VMEM,
        scratch_shapes=[pltpu.VMEM(small.shape, jnp.float32)],
        compiler_params=pltpu.CompilerParams(vmem_limit_bytes=16 * MIB),
        cost_estimate=pl.CostEstimate(flops=MIB, bytes_accessed=MIB, transcendentals=0),
        name="finish",
    )(queries, new_kv, *sums, partials)

    pair = cores == 2
    width = out_weight.shape[1] // (cores if pair else 1)
    partial = jax.ShapeDtypeStruct((rows, width), jnp.float32)
    mix = jax.ShapeDtypeStruct((rows, blocks * LANES), jnp.bfloat16)
    projected = pl.pallas_call(
        project_kernel,
        out_shape=(partial, mix) if pair else (partial,),
        in_specs=[VMEM] * 4,
        out_specs=(VMEM, VMEM) if pair else (VMEM,),
        compiler_params=pltpu.CompilerParams(vmem_limit_bytes=16 * MIB),
        name="project",
    )(meta, home, far, out_weight)
    if not pair:
        return projected[0]
    other = lax.ppermute(projected[0], "tp", [(0, 1), (1, 0)])
    own = pl.pallas_call(
        own_kernel,
        out_shape=partial,
        in_specs=[VMEM, VMEM],
        out_specs=VMEM,
        compiler_params=pltpu.CompilerParams(vmem_limit_bytes=16 * MIB),
        cost_estimate=pl.CostEstimate(
            flops=2 * rows * out_weight.size, bytes_accessed=out_weight.size, transcendentals=0
        ),
        name="own",
    )(projected[1], out_weight)
    return (own + other).astype(jnp.bfloat16)


def per_device(queries, new_kv, home_cache, help_cache, lengths, split_at, helper_req, out_weight):
    groups, cores = lax.axis_size("grp"), lax.axis_size("tp")
    partner = helper_req[0].astype(jnp.uint32) // queries.shape[0]
    distance = jnp.bitwise_xor(lax.axis_index("grp").astype(jnp.uint32), partner).astype(jnp.int32)
    packed, meta, *early = pack(lengths, split_at, helper_req, queries, home_cache, groups)
    arrays = (packed, meta, early, queries, new_kv, home_cache, help_cache, out_weight)
    if groups > MAX_BRANCHES:
        out = attention(*arrays, lambda x: lax.all_gather(x, "grp")[partner], cores)
    else:

        def at_distance(k):
            pairs = [(g, g ^ k) for g in range(groups)]
            return lambda *xs: attention(*xs, lambda x: lax.ppermute(x, "grp", pairs), cores)

        branches = [at_distance(k) for k in reversed(range(1, groups))]
        out = lax.switch(groups - 1 - distance, branches, *arrays)
    if cores == 2:
        return out
    return lax.psum_scatter(out, "tp", scatter_dimension=1, tiled=True).astype(jnp.bfloat16)


def solution(mesh):
    return jax.shard_map(
        per_device,
        mesh=mesh,
        in_specs=(
            P("grp", "tp"),
            P("grp", None, "tp"),
            P("grp", None, "tp", None, None),
            P("grp", None, "tp", None, None),
            P("grp"),
            P("grp"),
            P("grp"),
            P("tp", None),
        ),
        out_specs=P("grp", "tp"),
        check_vma=False,
    )
```
